32 devices in a mesh: fsdp: 4 (over y, x), rep: 8 (over z, core).
Axes of the slice: x: 2, y: 2, z: 4, core: 2. Of those that a mesh axis runs over, the one named last changes fastest.
Arguments:
- grads: bfloat16 [4, 8, 2, 512, 512], P('fsdp', 'rep'), may hold values from -0.25 to 0.25
- targets: int32 [4, 8, 2], P(None, 'rep'), may hold values from 0 to 7, as said below
- left_factor: float32 [4, 8, 2, 512, 512], P('fsdp', 'rep'), as said below
- right_factor: float32 [4, 8, 2, 512, 512], P('fsdp', 'rep'), as said below
- left_root: bfloat16 [4, 8, 2, 512, 512], P('fsdp', 'rep'), as said below
- right_root: bfloat16 [4, 8, 2, 512, 512], P('fsdp', 'rep'), as said below
- refresh: int32 [4, 8, 2], P('fsdp', 'rep'), may hold values 0 or 1
- buddy_offset: int32 [4], P('fsdp'), may hold values from 1 to 7
Outputs:
- new_left: bfloat16 [4, 8, 2, 512, 512], P('fsdp', 'rep')
- new_right: bfloat16 [4, 8, 2, 512, 512], P('fsdp', 'rep')
- buddy_left: bfloat16 [4, 8, 2, 512, 512], P('fsdp', 'rep')
- buddy_right: bfloat16 [4, 8, 2, 512, 512], P('fsdp', 'rep')
- precond: bfloat16 [4, 8, 2, 512, 512], P('fsdp', 'rep')
The draws below stay inside these ranges and needn't reach their ends.
Inputs may be any that keep to these rules, and one draw needn't show every extreme that they name: `targets`: for each replica index r, the blocks (f, r, k) fill every (owner, slot) pair exactly once; one device sends at most 1 block to one owner, and some device does so. `left_factor`: symmetric and positive definite. `right_factor`: symmetric and positive definite. `left_root`: symmetric. `right_root`: symmetric.
All inputs are finite; a program needn't handle non-finite values. No bound on the sum of `refresh` on one device may be relied on, other than what follows from the above.
Results may differ from the reference program's by a relative error of at most 0.0057.
Values may be sent and summed in bfloat16 or wider, within the bound.
A program may use at most 128 MiB of HBM per device.

```python
import jax
import jax.numpy as jnp
from jax import lax

B = 512
BLK_DEV = 2
N_FSDP = 4
N_REP = 8


def factor_diagonal(key, lower, upper):
    share = jax.random.uniform(key, (N_FSDP, N_REP, BLK_DEV, B), jnp.float32)
    return lower * (upper / lower) ** share


def symmetric_noise(key, spread):
    raw = jax.random.uniform(key, (N_FSDP, N_REP, BLK_DEV, B, B), jnp.float32, -spread, spread)
    return 0.5 * (raw + jnp.swapaxes(raw, -1, -2))


def with_diagonal(noise, values):
    identity = jnp.eye(B, dtype=jnp.float32)
    return noise * (1.0 - identity) + values[..., :, None] * identity


def draw_left_factor(key, part):
    values = factor_diagonal(jax.random.fold_in(key, 11), 3.0, 8.0)
    key = jax.random.fold_in(key, 1)
    return with_diagonal(symmetric_noise(key, 2.4 / B ** 0.5), values)


def draw_left_root(key, part):
    values = factor_diagonal(jax.random.fold_in(key, 11), 3.0, 8.0)
    key = jax.random.fold_in(key, 2)
    return with_diagonal(symmetric_noise(key, 0.3 / B ** 0.5), values ** (-0.25)).astype(jnp.bfloat16)


def draw_right_factor(key, part):
    values = factor_diagonal(jax.random.fold_in(key, 12), 3.0, 8.0)
    key = jax.random.fold_in(key, 3)
    return with_diagonal(symmetric_noise(key, 2.4 / B ** 0.5), values)


def draw_right_root(key, part):
    values = factor_diagonal(jax.random.fold_in(key, 12), 3.0, 8.0)
    key = jax.random.fold_in(key, 4)
    return with_diagonal(symmetric_noise(key, 0.3 / B ** 0.5), values ** (-0.25)).astype(jnp.bfloat16)


def draw_targets(key, part):
    key = jax.random.fold_in(key, 5)
    key_perm, key_shift, key_slot = jax.random.split(key, 3)
    owner_perm = jax.vmap(lambda sub: jax.random.permutation(sub, N_FSDP))(jax.random.split(key_perm, N_REP))
    shifts = jax.random.randint(key_shift, (N_REP,), 0, N_FSDP)
    slot_perm = jax.vmap(lambda sub: jax.random.permutation(sub, BLK_DEV))(jax.random.split(key_slot, N_REP))
    blocks = jnp.arange(BLK_DEV, dtype=jnp.int32)
    owner = (jnp.transpose(owner_perm)[:, :, None] + blocks[None, None, :] + shifts[None, :, None]) % N_FSDP
    slots = jnp.broadcast_to(slot_perm[None, :, :], (N_FSDP, N_REP, BLK_DEV))
    return (owner * BLK_DEV + slots).astype(jnp.int32)


def with_ends(entries, own_key, low, largest):
    extent = entries.shape
    spot = [jax.random.randint(jax.random.fold_in(own_key, axis), (), 0, extent[axis]) for axis in range(len(extent))]
    entries = entries.at[tuple(spot)].set(low)
    longest = extent.index(max(extent))
    spot[longest] = (spot[longest] + 1) % extent[longest]
    return entries.at[tuple(spot)].set(largest)


def block_scale(rng, shape, cuts, least, largest):
    def one(dim, shards_of):
        steps = jax.random.uniform(jax.random.fold_in(jax.random.fold_in(rng, 6), dim), (shards_of,), jnp.float32, least / len(cuts), largest / len(cuts))
        return jnp.repeat(jnp.exp(steps), shape[dim] // shards_of).reshape((-1,) + (1,) * (len(shape) - dim - 1))

    loudness = one(*cuts[0])
    for cut in cuts[1:]:
        loudness = loudness * one(*cut)
    return loudness


def bell_draw(own_key, dims, deviation, most, pieces=(), kind=jnp.bfloat16):
    array = jax.random.normal(own_key, dims, jnp.float32) * deviation
    if len(pieces) > 0:
        array = block_scale(own_key, dims, pieces, -0.22, 0.18) * array
    return jnp.clip(array, min=-most, max=most).astype(kind)


def setup_inputs(seed: int = 0) -> dict:
    splits = jax.random.split(jax.random.key(seed), 9)
    grads = bell_draw(splits[0], (N_FSDP, N_REP, BLK_DEV, B, B), B ** -0.5, 0.25, ((0, 4), (1, 8)))
    targets = draw_targets(jax.random.fold_in(splits[8], 71), 0)
    left_factor = draw_left_factor(jax.random.fold_in(splits[8], 71), 0)
    right_factor = draw_right_factor(jax.random.fold_in(splits[8], 71), 0)
    left_root = draw_left_root(jax.random.fold_in(splits[8], 71), 0)
    right_root = draw_right_root(jax.random.fold_in(splits[8], 71), 0)
    refresh = with_ends((jax.random.randint(splits[6], (N_FSDP, N_REP, BLK_DEV), 0, 2) < 1).astype(jnp.int32), jax.random.fold_in(splits[6], 1), 0, 1)
    buddy_offset = with_ends(jax.random.randint(splits[7], (N_FSDP,), 1, N_REP), jax.random.fold_in(splits[7], 1), 1, N_REP - 1).astype(jnp.int32)
    return dict(grads=grads, targets=targets, left_factor=left_factor, right_factor=right_factor, left_root=left_root, right_root=right_root, refresh=refresh, buddy_offset=buddy_offset)


def newton(factor, root):
    high = lax.Precision.HIGHEST
    square = jnp.dot(root, root, precision=high)
    fourth = jnp.dot(square, square, precision=high)
    moment = jnp.dot(fourth, factor, precision=high)
    return (5.0 * root - jnp.dot(root, moment, precision=high)) / 4.0


def reference(grads, targets, left_factor, right_factor, left_root, right_root, refresh, buddy_offset):
    width = grads.shape[-1]
    per_dev = targets.shape[2]
    owner = targets // per_dev
    slot = targets % per_dev
    rep_ids = jnp.arange(N_REP, dtype=jnp.int32)[None, :, None]
    flat_slot = ((owner * N_REP + rep_ids) * per_dev + slot).astype(jnp.int32).reshape(-1)
    total = flat_slot.shape[0]
    source = jnp.zeros((total,), jnp.int32).at[flat_slot].set(jnp.arange(total, dtype=jnp.int32))
    grad_flat = grads.reshape(total, width, width)
    left_flat = left_factor.reshape(total, width, width)
    right_flat = right_factor.reshape(total, width, width)
    lroot_flat = left_root.reshape(total, width, width)
    rroot_flat = right_root.reshape(total, width, width)
    mask_flat = refresh.reshape(total)

    def one_slot(index):
        block = grad_flat[source[index]]
        lfac = left_flat[index] + jnp.dot(block, block.T, preferred_element_type=jnp.float32)
        rfac = right_flat[index] + jnp.dot(block.T, block, preferred_element_type=jnp.float32)
        lold = lroot_flat[index].astype(jnp.float32)
        rold = rroot_flat[index].astype(jnp.float32)
        flag = mask_flat[index] == 1
        lnew = jnp.where(flag, newton(lfac, lold), lold).astype(jnp.bfloat16)
        rnew = jnp.where(flag, newton(rfac, rold), rold).astype(jnp.bfloat16)
        half = jnp.dot(lnew, block, preferred_element_type=jnp.float32).astype(jnp.bfloat16)
        result = jnp.dot(half, rnew, preferred_element_type=jnp.float32).astype(jnp.bfloat16)
        return lnew, rnew, result

    lnew, rnew, result = lax.map(one_slot, jnp.arange(total, dtype=jnp.int32))
    shape = grads.shape
    new_left = lnew.reshape(shape)
    new_right = rnew.reshape(shape)
    precond = result[flat_slot].reshape(shape)
    partner = jnp.bitwise_xor(jnp.arange(N_REP, dtype=jnp.int32)[None, :], buddy_offset[:, None]).astype(jnp.int32)
    pick = partner[:, :, None, None, None]
    buddy_left = jnp.take_along_axis(new_left, pick, axis=1)
    buddy_right = jnp.take_along_axis(new_right, pick, axis=1)
    return new_left, new_right, buddy_left, buddy_right, precond
```

```python
import functools

import jax
import jax.numpy as jnp
from jax import lax
from jax.experimental import pallas as pl
from jax.experimental.pallas import tpu as pltpu
from jax.sharding import PartitionSpec as P

MESH = pl.DeviceIdType.MESH
CUTS = 4
AHEAD = 2


def flip(index, mask):
    bit = 1
    while bit <= mask:
        if mask & bit:
            index = index + bit - 2 * bit * ((index // bit) % 2)
        bit *= 2
    return index


def mm(left, right):
    return jnp.dot(left, right, preferred_element_type=jnp.float32)


def split(value):
    high = value.astype(jnp.bfloat16)
    low = (value - high.astype(jnp.float32)).astype(jnp.bfloat16)
    return high, low


def mm3(left, right):
    (lh, ll), (rh, rl) = left, right
    return mm(lh, rh) + (mm(lh, rl) + mm(ll, rh))


def kernel(
    groups,
    replicas,
    targets,
    refresh,
    offset,
    grads,
    lfac_hbm,
    rfac_hbm,
    lroot_hbm,
    rroot_hbm,
    nleft_hbm,
    nright_hbm,
    bleft_hbm,
    bright_hbm,
    precond_hbm,
    fac,
    root,
    fifth_hi,
    fifth_lo,
    send_g,
    recv_g,
    owned,
    fresh,
    result,
    send_r,
    recv_r,
    home,
    moved,
    in_sem,
    out_sem,
    buddy_out_sem,
    g_send,
    g_recv,
    r_send,
    r_recv,
    b_send,
    b_recv,
):
    per, width = grads.shape[0], grads.shape[1]
    me = lax.axis_index("fsdp")
    rep = lax.axis_index("rep")
    levels = replicas.bit_length() - 1
    rows = width // CUTS
    chunks = 2 * per * CUTS

    loads = []
    for s in range(per):
        for side, (f_hbm, x_hbm) in enumerate(((lfac_hbm, lroot_hbm), (rfac_hbm, rroot_hbm))):
            m = 2 * s + side
            loads.append(pltpu.make_async_copy(x_hbm.at[s], root.at[m], in_sem.at[0, m]))
            loads.append(pltpu.make_async_copy(f_hbm.at[s], fac.at[m], in_sem.at[1, m]))
    for load in loads:
        load.start()

    barrier = pltpu.get_barrier_semaphore()
    for j in range(1, groups):
        pl.semaphore_signal(barrier, inc=1, device_id=(flip(me, j), rep), device_id_type=MESH)
    for level in range(levels):
        pl.semaphore_signal(
            barrier, inc=1, device_id=(me, flip(rep, 1 << level)), device_id_type=MESH
        )

    def block_for(owner):
        index = jnp.int32(0)
        for k in range(1, per):
            index = jnp.where(targets[me, 0, k] // per == owner, k, index)
        return index

    order = sorted(range(1, groups), key=lambda j: -bin(j).count("1"))
    for j in order:
        send_g[j] = grads[block_for(flip(me, j))]
    pl.semaphore_wait(barrier, groups - 1 + levels)

    def exchange(source, target, send_sem, recv_sem, j):
        return pltpu.make_async_remote_copy(
            src_ref=source.at[j],
            dst_ref=target.at[j],
            send_sem=send_sem.at[j],
            recv_sem=recv_sem.at[j],
            device_id=(flip(me, j), rep),
            device_id_type=MESH,
        )

    outward = [exchange(send_g, recv_g, g_send, g_recv, j) for j in order]
    for copy in outward:
        copy.start()
    recv_g[0] = grads[block_for(me)]
    for load in loads:
        load.wait()

    def powers(m, carry):
        x = root[m]
        square = split(mm(x, x))
        fourth = split(mm3(square, square))
        hi, lo = split(mm(x, fourth[0]) + mm(x, fourth[1]))
        fifth_hi[m] = hi
        fifth_lo[m] = lo
        return carry

    lax.fori_loop(0, 2 * per, powers, 0)
    for copy in outward:
        copy.wait_recv()

    for s in range(per):
        place = jnp.int32(0)
        for j in range(1, groups):
            source = flip(me, j)
            for k in range(per):
                place = jnp.where(targets[source, 0, k] == me * per + s, j, place)
        owned[s] = recv_g[place]

    def buddy_copy(level_no, c):
        level = levels - 1 - level_no
        source = fresh if level_no == 0 else moved.at[level_no - 1]
        m, cut = c // CUTS, pl.multiple_of((c % CUTS) * rows, rows)
        return pltpu.make_async_remote_copy(
            src_ref=source.at[m, pl.ds(cut, rows)],
            dst_ref=moved.at[level_no, m, pl.ds(cut, rows)],
            send_sem=b_send.at[level_no, c],
            recv_sem=b_recv.at[level_no, c],
            device_id=(me, flip(rep, 1 << level)),
            device_id_type=MESH,
        )

    def newton(m, s, gram):
        factor = split(fac[m] + gram)
        moment = mm3((fifth_hi[m], fifth_lo[m]), factor)
        old = root[m].astype(jnp.float32)
        new = (5.0 * old - moment) / 4.0
        fresh[m] = jnp.where(refresh[0, 0, s] == 1, new, old).astype(jnp.bfloat16)

    stores = []
    for s in range(per):
        block = owned[s]
        newton(
            2 * s,
            s,
            lax.dot_general(block, block, (((1,), (1,)), ((), ())), preferred_element_type=jnp.float32),
        )
        if s == 0:
            for c in range(AHEAD):
                buddy_copy(0, c).start()
        newton(
            2 * s + 1,
            s,
            lax.dot_general(block, block, (((0,), (0,)), ((), ())), preferred_element_type=jnp.float32),
        )
        half = mm(fresh[2 * s], block).astype(jnp.bfloat16)
        result[s] = mm(half, fresh[2 * s + 1]).astype(jnp.bfloat16)
        for side, out in enumerate((nleft_hbm, nright_hbm)):
            m = 2 * s + side
            stores.append(pltpu.make_async_copy(fresh.at[m], out.at[s], out_sem.at[m]))
            stores[-1].start()

    for j in [0] + order:
        index = jnp.int32(0)
        for k in range(per):
            there = targets[flip(me, j), 0, k]
            index = jnp.where(there // per == me, there % per, index)
        if j == 0:
            recv_r[0] = result[index]
        else:
            send_r[j] = result[index]
    backward = [exchange(send_r, recv_r, r_send, r_recv, j) for j in order]
    for copy in backward:
        copy.start()

    def buddy_store(c, wait):
        s, cut = c // (2 * CUTS), pl.multiple_of((c % CUTS) * rows, rows)
        for side, out in enumerate((bleft_hbm, bright_hbm)):

            @pl.when((c // CUTS) % 2 == side)
            def _():
                copy = pltpu.make_async_copy(
                    moved.at[levels - 1, 2 * s + side, pl.ds(cut, rows)],
                    out.at[s, pl.ds(cut, rows)],
                    buddy_out_sem.at[c],
                )
                if wait:
                    copy.wait()
                else:
                    copy.start()

    def step(t, carry):
        @pl.when(t < chunks)
        def _():
            buddy_copy(0, t).start()

        for n in range(levels):
            c = t - AHEAD - n

            @pl.when(jnp.logical_and(c >= 0, c < chunks))
            def _():
                buddy_copy(n, c).wait_recv()
                m, cut = c // CUTS, pl.multiple_of((c % CUTS) * rows, rows)
                level = levels - 1 - n
                crossing = (offset[0] // (1 << level)) % 2 == 1
                here = fresh if n == 0 else moved.at[n - 1]
                mine = here[m, pl.ds(cut, rows)].astype(jnp.float32)
                theirs = moved[n, m, pl.ds(cut, rows)].astype(jnp.float32)
                moved[n, m, pl.ds(cut, rows)] = jnp.where(crossing, theirs, mine).astype(
                    jnp.bfloat16
                )
                if n < levels - 1:
                    buddy_copy(n + 1, c).start()
                else:
                    buddy_store(c, False)

        return carry

    lax.fori_loop(AHEAD, chunks, step, 0)

    for copy in backward:
        copy.wait_recv()
    for k in range(per):
        place = jnp.int32(0)
        for j in range(1, groups):
            place = jnp.where(targets[me, 0, k] // per == flip(me, j), j, place)
        home[k] = recv_r[place]
    stores.append(pltpu.make_async_copy(home, precond_hbm, out_sem.at[2 * per]))
    stores[-1].start()

    lax.fori_loop(chunks, chunks + AHEAD + levels - 1, step, 0)

    for copy in stores:
        copy.wait()
    for copy in outward + backward:
        copy.wait_send()

    def drain(c, carry):
        for n in range(levels):
            buddy_copy(n, c).wait_send()
        buddy_store(c, True)
        return carry

    lax.fori_loop(0, chunks, drain, 0)


def per_device(
    groups,
    replicas,
    grads,
    targets,
    left_factor,
    right_factor,
    left_root,
    right_root,
    refresh,
    buddy_offset,
):
    per, width = grads.shape[2], grads.shape[3]
    levels = replicas.bit_length() - 1
    chunks = 2 * per * CUTS
    shape = grads.shape
    blocks = (per, width, width)
    bf = jnp.bfloat16
    smem = pl.BlockSpec(memory_space=pltpu.SMEM)
    vmem = pl.BlockSpec(memory_space=pltpu.VMEM)
    hbm = pl.BlockSpec(memory_space=pl.ANY)
    dma = pltpu.SemaphoreType.DMA
    matrices = (2 * per, width, width)
    slots = (groups, width, width)
    products = 2 * per * 10 + 2 * per
    outs = pl.pallas_call(
        functools.partial(kernel, groups, replicas),
        out_shape=[jax.ShapeDtypeStruct(blocks, bf)] * 5,
        in_specs=[smem, smem, smem, vmem, hbm, hbm, hbm, hbm],
        out_specs=[hbm] * 5,
        scratch_shapes=[
            pltpu.VMEM(matrices, jnp.float32),
            pltpu.VMEM(matrices, bf),
            pltpu.VMEM(matrices, bf),
            pltpu.VMEM(matrices, bf),
            pltpu.VMEM(slots, bf),
            pltpu.VMEM(slots, bf),
            pltpu.VMEM(blocks, bf),
            pltpu.VMEM(matrices, bf),
            pltpu.VMEM(blocks, bf),
            pltpu.VMEM(slots, bf),
            pltpu.VMEM(slots, bf),
            pltpu.VMEM(blocks, bf),
            pltpu.VMEM((levels,) + matrices, bf),
            dma((2, 2 * per)),
            dma((2 * per + 1,)),
            dma((chunks,)),
            dma((groups,)),
            dma((groups,)),
            dma((groups,)),
            dma((groups,)),
            dma((levels, chunks)),
            dma((levels, chunks)),
        ],
        compiler_params=pltpu.CompilerParams(
            collective_id=0, has_side_effects=True, vmem_limit_bytes=56 * 1024 * 1024
        ),
        cost_estimate=pl.CostEstimate(
            flops=products * 2 * width**3, bytes_accessed=24 * per * width**2, transcendentals=0
        ),
        name="refresh_and_exchange",
    )(
        targets,
        refresh,
        buddy_offset,
        grads.reshape(blocks),
        left_factor.reshape(blocks),
        right_factor.reshape(blocks),
        left_root.reshape(blocks),
        right_root.reshape(blocks),
    )
    return tuple(out.reshape(shape) for out in outs)


def solution(mesh):
    blocks = P("fsdp", "rep", None, None, None)
    placed = (
        blocks,
        P(None, "rep", None),
        blocks,
        blocks,
        blocks,
        blocks,
        P("fsdp", "rep", None),
        P("fsdp"),
    )
    return jax.shard_map(
        functools.partial(per_device, mesh.shape["fsdp"], mesh.shape["rep"]),
        mesh=mesh,
        in_specs=placed,
        out_specs=(blocks,) * 5,
        check_vma=False,
    )
```

```python
import functools

import jax
import jax.numpy as jnp
from jax import lax
from jax.experimental import pallas as pl
from jax.experimental.pallas import tpu as pltpu
from jax.sharding import PartitionSpec as P

MESH = pl.DeviceIdType.MESH
CUTS = 8
AHEAD = 3


def flip(index, mask):
    bit = 1
    while bit <= mask:
        if mask & bit:
            index = index + bit - 2 * bit * ((index // bit) % 2)
        bit *= 2
    return index


def mm(left, right):
    return jnp.dot(left, right, preferred_element_type=jnp.float32)


def split(value):
    high = value.astype(jnp.bfloat16)
    low = (value - high.astype(jnp.float32)).astype(jnp.bfloat16)
    return high, low


def mm3(left, right):
    (lh, ll), (rh, rl) = left, right
    return mm(lh, rh) + (mm(lh, rl) + mm(ll, rh))


def kernel(
    groups,
    replicas,
    targets,
    refresh,
    offset,
    grads,
    lfac_hbm,
    rfac_hbm,
    lroot_hbm,
    rroot_hbm,
    nleft_hbm,
    nright_hbm,
    bleft_hbm,
    bright_hbm,
    precond_hbm,
    fac,
    root,
    fifth_hi,
    fifth_lo,
    send_g,
    recv_g,
    owned,
    fresh,
    result,
    send_r,
    recv_r,
    home,
    moved,
    in_sem,
    out_sem,
    buddy_out_sem,
    g_send,
    g_recv,
    r_send,
    r_recv,
    b_send,
    b_recv,
):
    per, width = grads.shape[0], grads.shape[1]
    me = lax.axis_index("fsdp")
    rep = lax.axis_index("rep")
    levels = replicas.bit_length() - 1
    rows = width // CUTS
    chunks = 2 * per * CUTS

    loads = []
    for s in range(per):
        for side, (f_hbm, x_hbm) in enumerate(((lfac_hbm, lroot_hbm), (rfac_hbm, rroot_hbm))):
            m = 2 * s + side
            loads.append(pltpu.make_async_copy(x_hbm.at[s], root.at[m], in_sem.at[0, m]))
            loads.append(pltpu.make_async_copy(f_hbm.at[s], fac.at[m], in_sem.at[1, m]))
    for load in loads:
        load.start()

    barrier = pltpu.get_barrier_semaphore()
    for j in range(1, groups):
        pl.semaphore_signal(barrier, inc=1, device_id=(flip(me, j), rep), device_id_type=MESH)
    for level in range(levels):
        pl.semaphore_signal(
            barrier, inc=1, device_id=(me, flip(rep, 1 << level)), device_id_type=MESH
        )

    def block_for(owner):
        index = jnp.int32(0)
        for k in range(1, per):
            index = jnp.where(targets[k, me] // per == owner, k, index)
        return index

    order = sorted(range(1, groups), key=lambda j: -bin(j).count("1"))
    for j in order:
        send_g[j] = grads[block_for(flip(me, j))]
    pl.semaphore_wait(barrier, groups - 1 + levels)

    def exchange(source, target, send_sem, recv_sem, j):
        return pltpu.make_async_remote_copy(
            src_ref=source.at[j],
            dst_ref=target.at[j],
            send_sem=send_sem.at[j],
            recv_sem=recv_sem.at[j],
            device_id=(flip(me, j), rep),
            device_id_type=MESH,
        )

    outward = [exchange(send_g, recv_g, g_send, g_recv, j) for j in order]
    for copy in outward:
        copy.start()
    recv_g[0] = grads[block_for(me)]
    for load in loads:
        load.wait()

    def powers(m, carry):
        x = root[m]
        square = split(mm(x, x))
        fourth = split(mm3(square, square))
        hi, lo = split(mm(x, fourth[0]) + mm(x, fourth[1]))
        fifth_hi[m] = hi
        fifth_lo[m] = lo
        return carry

    lax.fori_loop(0, 2 * per, powers, 0)
    for copy in outward:
        copy.wait_recv()

    for s in range(per):
        place = jnp.int32(0)
        for j in range(1, groups):
            source = flip(me, j)
            for k in range(per):
                place = jnp.where(targets[k, source] == me * per + s, j, place)
        owned[s] = recv_g[place]

    def buddy_copy(level_no, c):
        level = levels - 1 - level_no
        source = fresh if level_no == 0 else moved.at[level_no - 1]
        m, cut = c // CUTS, pl.multiple_of((c % CUTS) * rows, rows)
        return pltpu.make_async_remote_copy(
            src_ref=source.at[m, pl.ds(cut, rows)],
            dst_ref=moved.at[level_no, m, pl.ds(cut, rows)],
            send_sem=b_send.at[level_no, c],
            recv_sem=b_recv.at[level_no, c],
            device_id=(me, flip(rep, 1 << level)),
            device_id_type=MESH,
        )

    def newton(m, s, gram):
        factor = split(fac[m] + gram)
        moment = mm3((fifth_hi[m], fifth_lo[m]), factor)
        old = root[m].astype(jnp.float32)
        new = (5.0 * old - moment) / 4.0
        fresh[m] = jnp.where(refresh[s] == 1, new, old).astype(jnp.bfloat16)

    stores = []
    for s in range(per):
        block = owned[s]
        newton(
            2 * s,
            s,
            lax.dot_general(block, block, (((1,), (1,)), ((), ())), preferred_element_type=jnp.float32),
        )
        if s == 0:
            for c in range(AHEAD):
                buddy_copy(0, c).start()
        newton(
            2 * s + 1,
            s,
            lax.dot_general(block, block, (((0,), (0,)), ((), ())), preferred_element_type=jnp.float32),
        )
        half = mm(fresh[2 * s], block).astype(jnp.bfloat16)
        result[s] = mm(half, fresh[2 * s + 1]).astype(jnp.bfloat16)
        for side, out in enumerate((nleft_hbm, nright_hbm)):
            m = 2 * s + side
            stores.append(pltpu.make_async_copy(fresh.at[m], out.at[s], out_sem.at[m]))
            stores[-1].start()

    for j in [0] + order:
        index = jnp.int32(0)
        for k in range(per):
            there = targets[k, flip(me, j)]
            index = jnp.where(there // per == me, there % per, index)
        if j == 0:
            recv_r[0] = result[index]
        else:
            send_r[j] = result[index]
    backward = [exchange(send_r, recv_r, r_send, r_recv, j) for j in order]
    for copy in backward:
        copy.start()

    def buddy_store(c, wait):
        s, cut = c // (2 * CUTS), pl.multiple_of((c % CUTS) * rows, rows)
        for side, out in enumerate((bleft_hbm, bright_hbm)):

            @pl.when((c // CUTS) % 2 == side)
            def _():
                copy = pltpu.make_async_copy(
                    moved.at[levels - 1, 2 * s + side, pl.ds(cut, rows)],
                    out.at[s, pl.ds(cut, rows)],
                    buddy_out_sem.at[c],
                )
                if wait:
                    copy.wait()
                else:
                    copy.start()

    def step(t, carry):
        @pl.when(t < chunks)
        def _():
            buddy_copy(0, t).start()

        for n in range(levels):
            c = t - AHEAD - n

            @pl.when(jnp.logical_and(c >= 0, c < chunks))
            def _():
                buddy_copy(n, c).wait_recv()
                m, cut = c // CUTS, pl.multiple_of((c % CUTS) * rows, rows)
                level = levels - 1 - n
                crossing = (offset[0] // (1 << level)) % 2 == 1
                here = fresh if n == 0 else moved.at[n - 1]
                mine = here[m, pl.ds(cut, rows)].astype(jnp.float32)
                theirs = moved[n, m, pl.ds(cut, rows)].astype(jnp.float32)
                moved[n, m, pl.ds(cut, rows)] = jnp.where(crossing, theirs, mine).astype(
                    jnp.bfloat16
                )
                if n < levels - 1:
                    buddy_copy(n + 1, c).start()
                else:
                    buddy_store(c, False)

        return carry

    lax.fori_loop(AHEAD, chunks, step, 0)

    for copy in backward:
        copy.wait_recv()
    for k in range(per):
        place = jnp.int32(0)
        for j in range(1, groups):
            place = jnp.where(targets[k, me] // per == flip(me, j), j, place)
        home[k] = recv_r[place]
    stores.append(pltpu.make_async_copy(home, precond_hbm, out_sem.at[2 * per]))
    stores[-1].start()

    lax.fori_loop(chunks, chunks + AHEAD + levels - 1, step, 0)

    for copy in stores:
        copy.wait()
    for copy in outward + backward:
        copy.wait_send()

    def drain(c, carry):
        for n in range(levels):
            buddy_copy(n, c).wait_send()
        buddy_store(c, True)
        return carry

    lax.fori_loop(0, chunks, drain, 0)


def hand_on(*refs):
    sources, targets, sem = refs[:5], refs[5:10], refs[10]
    copies = []
    for i in range(5):
        for half in range(2):
            part = pl.ds(half, 1) if sources[i].shape[0] == 2 else pl.ds(0, sources[i].shape[0])
            copies.append(
                pltpu.make_async_copy(sources[i].at[part], targets[i].at[part], sem.at[i, half])
            )
    for copy in copies:
        copy.start()
    for copy in copies:
        copy.wait()


def per_device(
    groups,
    replicas,
    grads,
    targets,
    left_factor,
    right_factor,
    left_root,
    right_root,
    refresh,
    buddy_offset,
):
    per, width = grads.shape[2], grads.shape[3]
    levels = replicas.bit_length() - 1
    chunks = 2 * per * CUTS
    shape = grads.shape
    blocks = (per, width, width)
    bf = jnp.bfloat16
    smem = pl.BlockSpec(memory_space=pltpu.SMEM)
    vmem = pl.BlockSpec(memory_space=pltpu.VMEM)
    hbm = pl.BlockSpec(memory_space=pl.ANY)
    dma = pltpu.SemaphoreType.DMA
    matrices = (2 * per, width, width)
    slots = (groups, width, width)
    products = 2 * per * 10 + 2 * per
    outs = pl.pallas_call(
        functools.partial(kernel, groups, replicas),
        out_shape=[jax.ShapeDtypeStruct(blocks, bf)] * 5,
        in_specs=[smem, smem, smem, vmem, hbm, hbm, hbm, hbm],
        out_specs=[hbm] * 5,
        scratch_shapes=[
            pltpu.VMEM(matrices, jnp.float32),
            pltpu.VMEM(matrices, bf),
            pltpu.VMEM(matrices, bf),
            pltpu.VMEM(matrices, bf),
            pltpu.VMEM(slots, bf),
            pltpu.VMEM(slots, bf),
            pltpu.VMEM(blocks, bf),
            pltpu.VMEM(matrices, bf),
            pltpu.VMEM(blocks, bf),
            pltpu.VMEM(slots, bf),
            pltpu.VMEM(slots, bf),
            pltpu.VMEM(blocks, bf),
            pltpu.VMEM((levels,) + matrices, bf),
            dma((2, 2 * per)),
            dma((2 * per + 1,)),
            dma((chunks,)),
            dma((groups,)),
            dma((groups,)),
            dma((groups,)),
            dma((groups,)),
            dma((levels, chunks)),
            dma((levels, chunks)),
        ],
        compiler_params=pltpu.CompilerParams(
            collective_id=0, has_side_effects=True, vmem_limit_bytes=56 * 1024 * 1024
        ),
        cost_estimate=pl.CostEstimate(
            flops=products * 2 * width**3, bytes_accessed=24 * per * width**2, transcendentals=0
        ),
        name="refresh_and_exchange",
    )(
        targets.transpose(1, 2, 0).reshape(per, groups),
        refresh.reshape(per),
        buddy_offset,
        grads.reshape(blocks),
        left_factor.reshape(blocks),
        right_factor.reshape(blocks),
        left_root.reshape(blocks),
        right_root.reshape(blocks),
    )
    outs = pl.pallas_call(
        hand_on,
        out_shape=[jax.ShapeDtypeStruct(blocks, bf)] * 5,
        in_specs=[hbm] * 5,
        out_specs=[hbm] * 5,
        scratch_shapes=[dma((5, 2))],
        name="hand_on",
    )(*outs)
    return tuple(out.reshape(shape) for out in outs)


def solution(mesh):
    blocks = P("fsdp", "rep", None, None, None)
    placed = (
        blocks,
        P(None, "rep", None),
        blocks,
        blocks,
        blocks,
        blocks,
        P("fsdp", "rep", None),
        P("fsdp"),
    )
    return jax.shard_map(
        functools.partial(per_device, mesh.shape["fsdp"], mesh.shape["rep"]),
        mesh=mesh,
        in_specs=placed,
        out_specs=(blocks,) * 5,
        check_vma=False,
    )
```

```python
import functools

import jax
import jax.numpy as jnp
from jax import lax
from jax.experimental import pallas as pl
from jax.experimental.pallas import tpu as pltpu
from jax.sharding import PartitionSpec as P

MESH = pl.DeviceIdType.MESH
CUTS = 8
AHEAD = 4
BEHIND = 3


def flip(index, mask):
    bit = 1
    while bit <= mask:
        if mask & bit:
            index = index + bit - 2 * bit * ((index // bit) % 2)
        bit *= 2
    return index


def mm(left, right):
    return jnp.dot(left, right, preferred_element_type=jnp.float32)


def split(value):
    high = value.astype(jnp.bfloat16)
    low = (value - high.astype(jnp.float32)).astype(jnp.bfloat16)
    return high, low


def mm3(left, right):
    (lh, ll), (rh, rl) = left, right
    return mm(lh, rh) + (mm(lh, rl) + mm(ll, rh))


def kernel(
    groups,
    replicas,
    targets,
    refresh,
    offset,
    grads,
    lfac_hbm,
    rfac_hbm,
    lroot_hbm,
    rroot_hbm,
    nleft_hbm,
    nright_hbm,
    bleft_hbm,
    bright_hbm,
    precond_hbm,
    fac,
    root,
    fifth_hi,
    fifth_lo,
    send_g,
    recv_g,
    owned,
    fresh,
    result,
    send_r,
    recv_r,
    home,
    moved,
    in_sem,
    out_sem,
    buddy_out_sem,
    g_send,
    g_recv,
    r_send,
    r_recv,
    b_send,
    b_recv,
):
    per, width = grads.shape[0], grads.shape[1]
    me = lax.axis_index("fsdp")
    rep = lax.axis_index("rep")
    levels = replicas.bit_length() - 1
    rows = width // CUTS
    chunks = 2 * per * CUTS

    loads = []
    for s in range(per):
        for side, (f_hbm, x_hbm) in enumerate(((lfac_hbm, lroot_hbm), (rfac_hbm, rroot_hbm))):
            m = 2 * s + side
            loads.append(pltpu.make_async_copy(x_hbm.at[s], root.at[m], in_sem.at[0, m]))
            loads.append(pltpu.make_async_copy(f_hbm.at[s], fac.at[m], in_sem.at[1, m]))
    for load in loads:
        load.start()

    barrier = pltpu.get_barrier_semaphore()
    for j in range(1, groups):
        pl.semaphore_signal(barrier, inc=1, device_id=(flip(me, j), rep), device_id_type=MESH)
    for level in range(levels):
        pl.semaphore_signal(
            barrier, inc=1, device_id=(me, flip(rep, 1 << level)), device_id_type=MESH
        )

    def block_for(owner):
        index = jnp.int32(0)
        for k in range(1, per):
            index = jnp.where(targets[k, me] // per == owner, k, index)
        return index

    order = sorted(range(1, groups), key=lambda j: -bin(j).count("1"))
    for j in order:
        send_g[j] = grads[block_for(flip(me, j))]
    pl.semaphore_wait(barrier, groups - 1 + levels)

    def exchange(source, target, send_sem, recv_sem, j):
        return pltpu.make_async_remote_copy(
            src_ref=source.at[j],
            dst_ref=target.at[j],
            send_sem=send_sem.at[j],
            recv_sem=recv_sem.at[j],
            device_id=(flip(me, j), rep),
            device_id_type=MESH,
        )

    outward = [exchange(send_g, recv_g, g_send, g_recv, j) for j in order]
    for copy in outward:
        copy.start()
    recv_g[0] = grads[block_for(me)]
    for load in loads:
        load.wait()

    def powers(m, carry):
        x = root[m]
        square = split(mm(x, x))
        fourth = split(mm3(square, square))
        hi, lo = split(mm(x, fourth[0]) + mm(x, fourth[1]))
        fifth_hi[m] = hi
        fifth_lo[m] = lo
        return carry

    lax.fori_loop(0, 2 * per, powers, 0)
    for copy in outward:
        copy.wait_recv()

    for s in range(per):
        place = jnp.int32(0)
        for j in range(1, groups):
            source = flip(me, j)
            for k in range(per):
                place = jnp.where(targets[k, source] == me * per + s, j, place)
        owned[s] = recv_g[place]

    def buddy_copy(level_no, c):
        level = levels - 1 - level_no
        source = fresh if level_no == 0 else moved.at[level_no - 1]
        m, cut = c // CUTS, pl.multiple_of((c % CUTS) * rows, rows)
        return pltpu.make_async_remote_copy(
            src_ref=source.at[m, pl.ds(cut, rows)],
            dst_ref=moved.at[level_no, m, pl.ds(cut, rows)],
            send_sem=b_send.at[level_no, c],
            recv_sem=b_recv.at[level_no, c],
            device_id=(me, flip(rep, 1 << level)),
            device_id_type=MESH,
        )

    def newton(m, s, gram):
        factor = split(fac[m] + gram)
        moment = mm3((fifth_hi[m], fifth_lo[m]), factor)
        old = root[m].astype(jnp.float32)
        new = (5.0 * old - moment) / 4.0
        fresh[m] = jnp.where(refresh[s] == 1, new, old).astype(jnp.bfloat16)

    stores = []
    for s in range(per):
        block = owned[s]
        newton(
            2 * s,
            s,
            lax.dot_general(block, block, (((1,), (1,)), ((), ())), preferred_element_type=jnp.float32),
        )
        if s == 0:
            for c in range(AHEAD):
                buddy_copy(0, c).start()
        newton(
            2 * s + 1,
            s,
            lax.dot_general(block, block, (((0,), (0,)), ((), ())), preferred_element_type=jnp.float32),
        )
        half = mm(fresh[2 * s], block).astype(jnp.bfloat16)
        result[s] = mm(half, fresh[2 * s + 1]).astype(jnp.bfloat16)
        for side, out in enumerate((nleft_hbm, nright_hbm)):
            m = 2 * s + side
            stores.append(pltpu.make_async_copy(fresh.at[m], out.at[s], out_sem.at[m]))
            stores[-1].start()

    for j in [0] + order:
        index = jnp.int32(0)
        for k in range(per):
            there = targets[k, flip(me, j)]
            index = jnp.where(there // per == me, there % per, index)
        if j == 0:
            recv_r[0] = result[index]
        else:
            send_r[j] = result[index]
    backward = [exchange(send_r, recv_r, r_send, r_recv, j) for j in order]
    for copy in backward:
        copy.start()

    def buddy_store(c, wait):
        s, cut = c // (2 * CUTS), pl.multiple_of((c % CUTS) * rows, rows)
        for side, out in enumerate((bleft_hbm, bright_hbm)):

            @pl.when((c // CUTS) % 2 == side)
            def _():
                copy = pltpu.make_async_copy(
                    moved.at[levels - 1, 2 * s + side, pl.ds(cut, rows)],
                    out.at[s, pl.ds(cut, rows)],
                    buddy_out_sem.at[c],
                )
                if wait:
                    copy.wait()
                else:
                    copy.start()

    def step(t, carry):
        @pl.when(t < chunks)
        def _():
            buddy_copy(0, t).start()

        for n in range(levels):
            c = t - AHEAD - BEHIND * n

            @pl.when(jnp.logical_and(c >= 0, c < chunks))
            def _():
                buddy_copy(n, c).wait_recv()
                m, cut = c // CUTS, pl.multiple_of((c % CUTS) * rows, rows)
                level = levels - 1 - n
                crossing = (offset[0] // (1 << level)) % 2 == 1
                here = fresh if n == 0 else moved.at[n - 1]
                mine = here[m, pl.ds(cut, rows)].astype(jnp.float32)
                theirs = moved[n, m, pl.ds(cut, rows)].astype(jnp.float32)
                moved[n, m, pl.ds(cut, rows)] = jnp.where(crossing, theirs, mine).astype(
                    jnp.bfloat16
                )
                if n < levels - 1:
                    buddy_copy(n + 1, c).start()
                else:
                    buddy_store(c, False)

        return carry

    lax.fori_loop(AHEAD, chunks, step, 0)

    for copy in backward:
        copy.wait_recv()
    for k in range(per):
        place = jnp.int32(0)
        for j in range(1, groups):
            place = jnp.where(targets[k, me] // per == flip(me, j), j, place)
        home[k] = recv_r[place]
    stores.append(pltpu.make_async_copy(home, precond_hbm, out_sem.at[2 * per]))
    stores[-1].start()

    lax.fori_loop(chunks, chunks + AHEAD + BEHIND * (levels - 1), step, 0)

    for copy in stores:
        copy.wait()
    for copy in outward + backward:
        copy.wait_send()

    def drain(c, carry):
        for n in range(levels):
            buddy_copy(n, c).wait_send()
        buddy_store(c, True)
        return carry

    lax.fori_loop(0, chunks, drain, 0)


def hand_on(*refs):
    sources, targets, (stage, load_sem, store_sem) = refs[:5], refs[5:10], refs[10:]
    loads, stores = [], []
    for i in range(5):
        for s in range(sources[i].shape[0]):
            loads.append(
                pltpu.make_async_copy(sources[i].at[s], stage.at[i, s], load_sem.at[i, s])
            )
            stores.append(
                pltpu.make_async_copy(stage.at[i, s], targets[i].at[s], store_sem.at[i, s])
            )
    for load in loads:
        load.start()
    for load, store in zip(loads, stores):
        load.wait()
        store.start()
    for store in stores:
        store.wait()


def per_device(
    groups,
    replicas,
    grads,
    targets,
    left_factor,
    right_factor,
    left_root,
    right_root,
    refresh,
    buddy_offset,
):
    per, width = grads.shape[2], grads.shape[3]
    levels = replicas.bit_length() - 1
    chunks = 2 * per * CUTS
    shape = grads.shape
    blocks = (per, width, width)
    bf = jnp.bfloat16
    smem = pl.BlockSpec(memory_space=pltpu.SMEM)
    vmem = pl.BlockSpec(memory_space=pltpu.VMEM)
    hbm = pl.BlockSpec(memory_space=pl.ANY)
    dma = pltpu.SemaphoreType.DMA
    matrices = (2 * per, width, width)
    slots = (groups, width, width)
    products = 2 * per * 10 + 2 * per
    outs = pl.pallas_call(
        functools.partial(kernel, groups, replicas),
        out_shape=[jax.ShapeDtypeStruct(blocks, bf)] * 5,
        in_specs=[smem, smem, smem, vmem, hbm, hbm, hbm, hbm],
        out_specs=[hbm] * 5,
        scratch_shapes=[
            pltpu.VMEM(matrices, jnp.float32),
            pltpu.VMEM(matrices, bf),
            pltpu.VMEM(matrices, bf),
            pltpu.VMEM(matrices, bf),
            pltpu.VMEM(slots, bf),
            pltpu.VMEM(slots, bf),
            pltpu.VMEM(blocks, bf),
            pltpu.VMEM(matrices, bf),
            pltpu.VMEM(blocks, bf),
            pltpu.VMEM(slots, bf),
            pltpu.VMEM(slots, bf),
            pltpu.VMEM(blocks, bf),
            pltpu.VMEM((levels,) + matrices, bf),
            dma((2, 2 * per)),
            dma((2 * per + 1,)),
            dma((chunks,)),
            dma((groups,)),
            dma((groups,)),
            dma((groups,)),
            dma((groups,)),
            dma((levels, chunks)),
            dma((levels, chunks)),
        ],
        compiler_params=pltpu.CompilerParams(
            collective_id=0, has_side_effects=True, vmem_limit_bytes=56 * 1024 * 1024
        ),
        cost_estimate=pl.CostEstimate(
            flops=products * 2 * width**3, bytes_accessed=24 * per * width**2, transcendentals=0
        ),
        name="refresh_and_exchange",
    )(
        targets.transpose(1, 2, 0).reshape(per, groups),
        refresh.reshape(per),
        buddy_offset,
        grads.reshape(blocks),
        left_factor.reshape(blocks),
        right_factor.reshape(blocks),
        left_root.reshape(blocks),
        right_root.reshape(blocks),
    )
    outs = pl.pallas_call(
        hand_on,
        out_shape=[jax.ShapeDtypeStruct(blocks, bf)] * 5,
        in_specs=[hbm] * 5,
        out_specs=[hbm] * 5,
        scratch_shapes=[pltpu.VMEM((5,) + blocks, bf), dma((5, per)), dma((5, per))],
        name="hand_on",
    )(*outs)
    return tuple(out.reshape(shape) for out in outs)


def solution(mesh):
    blocks = P("fsdp", "rep", None, None, None)
    placed = (
        blocks,
        P(None, "rep", None),
        blocks,
        blocks,
        blocks,
        blocks,
        P("fsdp", "rep", None),
        P("fsdp"),
    )
    return jax.shard_map(
        functools.partial(per_device, mesh.shape["fsdp"], mesh.shape["rep"]),
        mesh=mesh,
        in_specs=placed,
        out_specs=(blocks,) * 5,
        check_vma=False,
    )
```

```python
import functools

import jax
import jax.numpy as jnp
from jax import lax
from jax.experimental import pallas as pl
from jax.experimental.pallas import tpu as pltpu
from jax.sharding import PartitionSpec as P

MESH = pl.DeviceIdType.MESH
CUTS = 8
PARTS = 16
AHEAD = 4
BEHIND = 3


def flip(index, mask):
    bit = 1
    while bit <= mask:
        if mask & bit:
            index = index + bit - 2 * bit * ((index // bit) % 2)
        bit *= 2
    return index


def mm(left, right):
    return jnp.dot(left, right, preferred_element_type=jnp.float32)


def split(value):
    high = value.astype(jnp.bfloat16)
    low = (value - high.astype(jnp.float32)).astype(jnp.bfloat16)
    return high, low


def mm3(left, right):
    (lh, ll), (rh, rl) = left, right
    return mm(lh, rh) + (mm(lh, rl) + mm(ll, rh))


def refresh_kernel(
    groups,
    targets,
    refresh,
    offset,
    grads,
    lfac_hbm,
    rfac_hbm,
    lroot_hbm,
    rroot_hbm,
    fresh_hbm,
    result_hbm,
    offsets_out,
    fac,
    root,
    fifth_hi,
    fifth_lo,
    send_g,
    recv_g,
    owned,
    fresh,
    result,
    offsets,
    in_sem,
    out_sem,
    g_send,
    g_recv,
    o_send,
    o_recv,
):
    per, width = grads.shape[0], grads.shape[1]
    me = lax.axis_index("fsdp")
    rep = lax.axis_index("rep")

    loads = []
    for s in range(per):
        for side, (f_hbm, x_hbm) in enumerate(((lfac_hbm, lroot_hbm), (rfac_hbm, rroot_hbm))):
            m = side * per + s
            loads.append(pltpu.make_async_copy(x_hbm.at[s], root.at[m], in_sem.at[0, m]))
            loads.append(pltpu.make_async_copy(f_hbm.at[s], fac.at[m], in_sem.at[1, m]))
    for load in loads:
        load.start()

    barrier = pltpu.get_barrier_semaphore()
    for j in range(1, groups):
        pl.semaphore_signal(barrier, inc=1, device_id=(flip(me, j), rep), device_id_type=MESH)

    def block_for(owner):
        index = jnp.int32(0)
        for k in range(1, per):
            index = jnp.where(targets[k, me] // per == owner, k, index)
        return index

    order = sorted(range(1, groups), key=lambda j: -bin(j).count("1"))
    for j in order:
        send_g[j] = grads[block_for(flip(me, j))]
    offsets[0] = jnp.full(offsets.shape[1:], offset[0], jnp.int32)
    pl.semaphore_wait(barrier, groups - 1)

    def exchange(source, j, target, send_sem, recv_sem):
        return pltpu.make_async_remote_copy(
            src_ref=source,
            dst_ref=target.at[j],
            send_sem=send_sem.at[j],
            recv_sem=recv_sem.at[j],
            device_id=(flip(me, j), rep),
            device_id_type=MESH,
        )

    outward = [exchange(offsets.at[0], j, offsets, o_send, o_recv) for j in order]
    outward += [exchange(send_g.at[j], j, recv_g, g_send, g_recv) for j in order]
    for copy in outward:
        copy.start()
    recv_g[0] = grads[block_for(me)]
    for load in loads:
        load.wait()

    def powers(m, carry):
        x = root[m]
        square = split(mm(x, x))
        fourth = split(mm3(square, square))
        hi, lo = split(mm(x, fourth[0]) + mm(x, fourth[1]))
        fifth_hi[m] = hi
        fifth_lo[m] = lo
        return carry

    lax.fori_loop(0, 2 * per, powers, 0)
    for copy in outward:
        copy.wait_recv()

    for s in range(per):
        place = jnp.int32(0)
        for j in range(1, groups):
            source = flip(me, j)
            for k in range(per):
                place = jnp.where(targets[k, source] == me * per + s, j, place)
        owned[s] = recv_g[place]

    def newton(m, s, gram):
        factor = split(fac[m] + gram)
        moment = mm3((fifth_hi[m], fifth_lo[m]), factor)
        old = root[m].astype(jnp.float32)
        new = (5.0 * old - moment) / 4.0
        fresh[m] = jnp.where(refresh[s] == 1, new, old).astype(jnp.bfloat16)

    def gram(block, dim):
        dims = (((dim,), (dim,)), ((), ()))
        return lax.dot_general(block, block, dims, preferred_element_type=jnp.float32)

    stores = []
    for s in range(per):
        block = owned[s]
        newton(s, s, gram(block, 1))
        newton(per + s, s, gram(block, 0))
        for m in (s, per + s):
            stores.append(pltpu.make_async_copy(fresh.at[m], fresh_hbm.at[m], out_sem.at[m]))
            stores[-1].start()
        half = mm(fresh[s], block).astype(jnp.bfloat16)
        result[s] = mm(half, fresh[per + s]).astype(jnp.bfloat16)
        stores.append(
            pltpu.make_async_copy(result.at[s], result_hbm.at[s], out_sem.at[2 * per + s])
        )
        stores[-1].start()
    offsets_out[...] = offsets[...]
    for copy in stores:
        copy.wait()
    for copy in outward:
        copy.wait_send()


def greet(peers):
    barrier = pltpu.get_barrier_semaphore()
    for peer in peers:
        pl.semaphore_signal(barrier, inc=1, device_id=peer, device_id_type=MESH)
    pl.semaphore_wait(barrier, len(peers))


def choose(condition, one, other):
    return jnp.where(condition, one.astype(jnp.float32), other.astype(jnp.float32)).astype(
        jnp.bfloat16
    )


class Homeward:
    def __init__(self, groups, targets, result, send, recv, send_sem, recv_sem):
        self.groups, self.per, self.targets = groups, result.shape[0], targets
        self.recv = recv
        self.me, self.rep = lax.axis_index("fsdp"), lax.axis_index("rep")
        self.order = sorted(range(1, groups), key=lambda j: -bin(j).count("1"))
        for j in [0] + self.order:
            index = jnp.int32(0)
            for k in range(self.per):
                there = targets[k, flip(self.me, j)]
                index = jnp.where(there // self.per == self.me, there % self.per, index)
            (recv if j == 0 else send)[j] = result[index]
        self.copies = [
            pltpu.make_async_remote_copy(
                src_ref=send.at[j],
                dst_ref=recv.at[j],
                send_sem=send_sem.at[j],
                recv_sem=recv_sem.at[j],
                device_id=(flip(self.me, j), self.rep),
                device_id_type=MESH,
            )
            for j in self.order
        ]

    def start(self):
        for copy in self.copies:
            copy.start()

    def finish(self, home):
        for copy in self.copies:
            copy.wait_recv()
        for k in range(self.per):
            place = jnp.int32(0)
            for j in range(1, self.groups):
                owner = self.targets[k, self.me] // self.per
                place = jnp.where(owner == flip(self.me, j), j, place)
            home[k] = self.recv[place]

    def wait_send(self):
        for copy in self.copies:
            copy.wait_send()


def butterfly_kernel(
    groups,
    replicas,
    offsets,
    targets,
    fresh,
    result,
    buddy_hbm,
    precond_hbm,
    send_r,
    recv_r,
    home,
    moved,
    store_sem,
    home_sem,
    r_send,
    r_recv,
    b_send,
    b_recv,
):
    matrices, width = fresh.shape[0], fresh.shape[1]
    me, rep = lax.axis_index("fsdp"), lax.axis_index("rep")
    levels = replicas.bit_length() - 1
    rows = width // CUTS
    chunks = matrices * CUTS
    greet(
        [(flip(me, j), rep) for j in range(1, groups)]
        + [(me, flip(rep, 1 << level)) for level in range(levels)]
    )
    homeward = Homeward(groups, targets, result, send_r, recv_r, r_send, r_recv)
    homeward.start()

    def spot(c):
        return c // CUTS, pl.ds(pl.multiple_of((c % CUTS) * rows, rows), rows)

    def buddy_copy(n, c):
        source = fresh if n == 0 else moved.at[n - 1]
        m, part = spot(c)
        return pltpu.make_async_remote_copy(
            src_ref=source.at[m, part],
            dst_ref=moved.at[n, m, part],
            send_sem=b_send.at[n, c],
            recv_sem=b_recv.at[n, c],
            device_id=(me, flip(rep, 1 << (levels - 1 - n))),
            device_id_type=MESH,
        )

    def buddy_store(c):
        m, part = spot(c)
        return pltpu.make_async_copy(
            moved.at[levels - 1, m, part], buddy_hbm.at[m, part], store_sem.at[c]
        )

    def step(t, carry):
        @pl.when(t < chunks)
        def _():
            buddy_copy(0, t).start()

        for n in range(levels):
            c = t - AHEAD - BEHIND * n

            @pl.when(jnp.logical_and(c >= 0, c < chunks))
            def _():
                buddy_copy(n, c).wait_recv()
                m, part = spot(c)
                crossing = (offsets[0] // (1 << (levels - 1 - n))) % 2 == 1
                here = fresh if n == 0 else moved.at[n - 1]
                moved[n, m, part] = choose(crossing, moved[n, m, part], here[m, part])
                if n < levels - 1:
                    buddy_copy(n + 1, c).start()
                else:
                    buddy_store(c).start()

        return carry

    lax.fori_loop(0, chunks, step, 0)
    homeward.finish(home)
    bring = pltpu.make_async_copy(home, precond_hbm, home_sem.at[0])
    bring.start()
    lax.fori_loop(chunks, chunks + AHEAD + BEHIND * (levels - 1), step, 0)
    bring.wait()
    homeward.wait_send()

    def drain(c, carry):
        for n in range(levels):
            buddy_copy(n, c).wait_send()
        buddy_store(c).wait()
        return carry

    lax.fori_loop(0, chunks, drain, 0)


def spread_kernel(
    offsets,
    targets,
    fresh,
    result,
    buddy_hbm,
    precond_hbm,
    send_r,
    recv_r,
    home,
    twin,
    ready,
    guest,
    far_out,
    far_in,
    far,
    near_out,
    near_in,
    near,
    back,
    store_sem,
    home_sem,
    r_send,
    r_recv,
    t_send,
    t_recv,
    g_send,
    g_recv,
    f_send,
    f_recv,
    n_send,
    n_recv,
    b_send,
    b_recv,
):
    groups, width = fresh.shape[0], fresh.shape[1]
    me, rep = lax.axis_index("fsdp"), lax.axis_index("rep")
    others = range(1, groups)
    rows = width // PARTS
    greet(
        [(flip(me, j), rep) for j in others] + [(me, flip(rep, 1 << level)) for level in range(3)]
    )

    def span(c):
        return pl.ds(pl.multiple_of(c * rows, rows), rows)

    def send(source, target, send_sem, recv_sem, device):
        return pltpu.make_async_remote_copy(
            src_ref=source,
            dst_ref=target,
            send_sem=send_sem,
            recv_sem=recv_sem,
            device_id=device,
            device_id_type=MESH,
        )

    def to_twin(c):
        part = (slice(None), span(c))
        return send(
            fresh.at[part], twin.at[part], t_send.at[c], t_recv.at[c], (me, flip(rep, 1))
        )

    def to_guest(j, c):
        part = (j, span(c))
        return send(
            ready.at[part], guest.at[part], g_send.at[j, c], g_recv.at[j, c], (flip(me, j), rep)
        )

    def to_far(c):
        part = (slice(None), span(c))
        return send(
            far_out.at[part], far_in.at[part], f_send.at[c], f_recv.at[c], (me, flip(rep, 4))
        )

    def to_near(c):
        part = (slice(None), span(c))
        return send(
            near_out.at[part], near_in.at[part], n_send.at[c], n_recv.at[c], (me, flip(rep, 2))
        )

    def to_home(j, c):
        part = (j, span(c))
        return send(
            near.at[part], back.at[part], b_send.at[j, c], b_recv.at[j, c], (flip(me, j), rep)
        )

    def to_hbm(c):
        part = (slice(None), span(c))
        return pltpu.make_async_copy(back.at[part], buddy_hbm.at[part], store_sem.at[c])

    def bit(j, mask):
        return (offsets[j] // mask) % 2 == 1

    def staying(mask):
        index = jnp.int32(0)
        for j in reversed(range(groups)):
            index = jnp.where(bit(j, mask), index, j)
        return index

    stays_far, stays_near = staying(4), staying(2)

    def pack(here, out, stays, part):
        for i in range(groups - 1):
            out[i, part] = choose(stays <= i, here(i + 1), here(i))

    def unpack(here, arrived, stays, mask, target, part):
        for j in range(groups):
            if j == 0:
                theirs = arrived[0, part]
            elif j == groups - 1:
                theirs = arrived[j - 1, part]
            else:
                theirs = choose(stays < j, arrived[j - 1, part], arrived[j, part])
            target[j, part] = choose(bit(j, mask), theirs, here(j))

    def step(t, carry):
        @pl.when(t < PARTS)
        def _():
            to_twin(t).start()

        def stage(lag, work):
            c = t - lag

            @pl.when(jnp.logical_and(c >= 0, c < PARTS))
            def _():
                work(c)

        def leave(c):
            to_twin(c).wait_recv()
            part = span(c)
            for j in reversed(range(groups)):
                ready[j, part] = choose(bit(0, 1), twin[j, part], fresh[j, part])
                if j > 0:
                    to_guest(j, c).start()

        def visit(part):
            return lambda j: (ready if j == 0 else guest)[j, part]

        def cross_far(c):
            for j in others:
                to_guest(j, c).wait_recv()
            part = span(c)
            pack(visit(part), far_out, stays_far, part)
            to_far(c).start()

        def cross_near(c):
            to_far(c).wait_recv()
            part = span(c)
            unpack(visit(part), far_in, stays_far, 4, far, part)
            pack(lambda j: far[j, part], near_out, stays_near, part)
            to_near(c).start()

        def go_home(c):
            to_near(c).wait_recv()
            part = span(c)
            unpack(lambda j: far[j, part], near_in, stays_near, 2, near, part)
            for j in others:
                to_home(j, c).start()
            back[0, part] = near[0, part]

        def arrive(c):
            for j in others:
                to_home(j, c).wait_recv()
            to_hbm(c).start()

        stage(2, leave)
        stage(4, cross_far)
        stage(6, cross_near)
        stage(8, go_home)
        stage(10, arrive)
        return carry

    lax.fori_loop(0, 4, step, 0)
    homeward = Homeward(groups, targets, result, send_r, recv_r, r_send, r_recv)
    homeward.start()
    lax.fori_loop(4, PARTS, step, 0)
    homeward.finish(home)
    bring = pltpu.make_async_copy(home, precond_hbm, home_sem.at[0])
    bring.start()
    lax.fori_loop(PARTS, PARTS + 10, step, 0)
    bring.wait()
    homeward.wait_send()

    def drain(c, carry):
        to_twin(c).wait_send()
        to_far(c).wait_send()
        to_near(c).wait_send()
        for j in others:
            to_guest(j, c).wait_send()
            to_home(j, c).wait_send()
        to_hbm(c).wait()
        return carry

    lax.fori_loop(0, PARTS, drain, 0)


def hand_on(fresh, buddy, precond, nleft, nright, bleft, bright, home, stage, load_sem, store_sem):
    per = precond.shape[0]
    loads, stores = [], []
    pairs = [(fresh, 0, nleft), (fresh, per, nright), (buddy, 0, bleft), (buddy, per, bright)]
    for i, (source, first, target) in enumerate(pairs + [(precond, 0, home)]):
        for s in range(per):
            loads.append(
                pltpu.make_async_copy(source.at[first + s], stage.at[i, s], load_sem.at[i, s])
            )
            stores.append(
                pltpu.make_async_copy(stage.at[i, s], target.at[s], store_sem.at[i, s])
            )
    for load in loads:
        load.start()
    for load, store in zip(loads, stores):
        load.wait()
        store.start()
    for store in stores:
        store.wait()


def per_device(
    groups,
    replicas,
    grads,
    targets,
    left_factor,
    right_factor,
    left_root,
    right_root,
    refresh,
    buddy_offset,
):
    per, width = grads.shape[2], grads.shape[3]
    levels = replicas.bit_length() - 1
    chunks = 2 * per * CUTS
    shape = grads.shape
    blocks = (per, width, width)
    matrices = (2 * per, width, width)
    slots = (groups, width, width)
    bf = jnp.bfloat16
    smem = pl.BlockSpec(memory_space=pltpu.SMEM)
    vmem = pl.BlockSpec(memory_space=pltpu.VMEM)
    hbm = pl.BlockSpec(memory_space=pl.ANY)
    dma = pltpu.SemaphoreType.DMA

    def held(dims, kind=bf):
        return pltpu.VMEM(dims, kind)

    def params(number):
        return pltpu.CompilerParams(
            collective_id=number, has_side_effects=True, vmem_limit_bytes=56 * 1024 * 1024
        )

    table = targets.transpose(1, 2, 0).reshape(per, groups)
    fresh, result, offsets = pl.pallas_call(
        functools.partial(refresh_kernel, groups),
        out_shape=[
            jax.ShapeDtypeStruct(matrices, bf),
            jax.ShapeDtypeStruct(blocks, bf),
            jax.ShapeDtypeStruct((groups, 8, 128), jnp.int32),
        ],
        in_specs=[smem, smem, smem, vmem, hbm, hbm, hbm, hbm],
        out_specs=[hbm, hbm, vmem],
        scratch_shapes=[
            held(matrices, jnp.float32),
            held(matrices),
            held(matrices),
            held(matrices),
            held(slots),
            held(slots),
            held(blocks),
            held(matrices),
            held(blocks),
            held((groups, 8, 128), jnp.int32),
            dma((2, 2 * per)),
            dma((3 * per,)),
            dma((groups,)),
            dma((groups,)),
            dma((groups,)),
            dma((groups,)),
        ],
        compiler_params=params(0),
        name="refresh",
    )(
        table,
        refresh.reshape(per),
        buddy_offset,
        grads.reshape(blocks),
        left_factor.reshape(blocks),
        right_factor.reshape(blocks),
        left_root.reshape(blocks),
        right_root.reshape(blocks),
    )
    offsets = offsets[:, 0, 0]

    def finish(body, number, name, scratch):
        return pl.pallas_call(
            body,
            out_shape=[jax.ShapeDtypeStruct(matrices, bf), jax.ShapeDtypeStruct(blocks, bf)],
            in_specs=[smem, smem, vmem, vmem],
            out_specs=[hbm, hbm],
            scratch_shapes=[held(slots), held(slots), held(blocks)] + scratch,
            compiler_params=params(number),
            name=name,
        )

    butterfly = finish(
        functools.partial(butterfly_kernel, groups, replicas),
        1,
        "butterfly",
        [
            held((levels,) + matrices),
            dma((chunks,)),
            dma((1,)),
            dma((groups,)),
            dma((groups,)),
            dma((levels, chunks)),
            dma((levels, chunks)),
        ],
    )
    inputs = (offsets, table, fresh, result)
    if groups == 4 and replicas == 8 and 2 * per == groups:
        moving = (groups - 1, width, width)
        each = [dma((PARTS,)), dma((PARTS,))]
        pairs = [dma((groups, PARTS)), dma((groups, PARTS))]
        spread = finish(
            spread_kernel,
            2,
            "spread",
            [held(matrices)] * 3
            + [held(moving)] * 2
            + [held(matrices)]
            + [held(moving)] * 2
            + [held(matrices)] * 2
            + [dma((PARTS,)), dma((1,)), dma((groups,)), dma((groups,))]
            + each
            + pairs
            + each
            + each
            + pairs,
        )
        far = jnp.sum((offsets // 4) % 2)
        near = jnp.sum((offsets // 2) % 2)
        buddy, home = lax.cond(
            jnp.logical_and(far < groups, near < groups),
            lambda *ins: spread(*ins),
            lambda *ins: butterfly(*ins),
            *inputs,
        )
    else:
        buddy, home = butterfly(*inputs)
    outs = pl.pallas_call(
        hand_on,
        out_shape=[jax.ShapeDtypeStruct(blocks, bf)] * 5,
        in_specs=[hbm] * 3,
        out_specs=[hbm] * 5,
        scratch_shapes=[held((5,) + blocks), dma((5, per)), dma((5, per))],
        name="hand_on",
    )(fresh, buddy, home)
    return tuple(out.reshape(shape) for out in outs)


def solution(mesh):
    blocks = P("fsdp", "rep", None, None, None)
    placed = (
        blocks,
        P(None, "rep", None),
        blocks,
        blocks,
        blocks,
        blocks,
        P("fsdp", "rep", None),
        P("fsdp"),
    )
    return jax.shard_map(
        functools.partial(per_device, mesh.shape["fsdp"], mesh.shape["rep"]),
        mesh=mesh,
        in_specs=placed,
        out_specs=(blocks,) * 5,
        check_vma=False,
    )
```

```python
import functools

import jax
import jax.numpy as jnp
from jax import lax
from jax.experimental import pallas as pl
from jax.experimental.pallas import tpu as pltpu
from jax.sharding import PartitionSpec as P

MESH = pl.DeviceIdType.MESH
CUTS = 8
AHEAD = 4
BEHIND = 3


def flip(index, mask):
    bit = 1
    while bit <= mask:
        if mask & bit:
            index = index + bit - 2 * bit * ((index // bit) % 2)
        bit *= 2
    return index


def mm(left, right):
    return jnp.dot(left, right, preferred_element_type=jnp.float32)


def split(value):
    high = value.astype(jnp.bfloat16)
    low = (value - high.astype(jnp.float32)).astype(jnp.bfloat16)
    return high, low


def mm3(left, right):
    (lh, ll), (rh, rl) = left, right
    return mm(lh, rh) + (mm(lh, rl) + mm(ll, rh))


def kernel(
    groups,
    replicas,
    targets,
    refresh,
    offset,
    grads_hbm,
    lfac_hbm,
    rfac_hbm,
    lroot_hbm,
    rroot_hbm,
    nleft_hbm,
    nright_hbm,
    bleft_hbm,
    bright_hbm,
    precond_hbm,
    grads,
    fac,
    root,
    fifth_hi,
    fifth_lo,
    send_g,
    recv_g,
    owned,
    fresh,
    result,
    send_r,
    recv_r,
    home,
    moved,
    in_sem,
    out_sem,
    buddy_out_sem,
    g_send,
    g_recv,
    r_send,
    r_recv,
    b_send,
    b_recv,
):
    per, width = grads.shape[0], grads.shape[1]
    me = lax.axis_index("fsdp")
    rep = lax.axis_index("rep")
    levels = replicas.bit_length() - 1
    rows = width // CUTS
    chunks = 2 * per * CUTS

    blocks_in = pltpu.make_async_copy(grads_hbm, grads, in_sem.at[2, 0])
    blocks_in.start()

    barrier = pltpu.get_barrier_semaphore()
    for j in range(1, groups):
        pl.semaphore_signal(barrier, inc=1, device_id=(flip(me, j), rep), device_id_type=MESH)
    for level in range(levels):
        pl.semaphore_signal(
            barrier, inc=1, device_id=(me, flip(rep, 1 << level)), device_id_type=MESH
        )

    loads = []
    for s in range(per):
        for side, (f_hbm, x_hbm) in enumerate(((lfac_hbm, lroot_hbm), (rfac_hbm, rroot_hbm))):
            m = 2 * s + side
            loads.append(pltpu.make_async_copy(x_hbm.at[s], root.at[m], in_sem.at[0, m]))
            loads.append(pltpu.make_async_copy(f_hbm.at[s], fac.at[m], in_sem.at[1, m]))
    for load in loads:
        load.start()

    def block_for(owner):
        index = jnp.int32(0)
        for k in range(1, per):
            index = jnp.where(targets[k, me] // per == owner, k, index)
        return index

    order = sorted(range(1, groups), key=lambda j: -bin(j).count("1"))
    def exchange(source, target, send_sem, recv_sem, j):
        return pltpu.make_async_remote_copy(
            src_ref=source.at[j],
            dst_ref=target.at[j],
            send_sem=send_sem.at[j],
            recv_sem=recv_sem.at[j],
            device_id=(flip(me, j), rep),
            device_id_type=MESH,
        )

    outward = [exchange(send_g, recv_g, g_send, g_recv, j) for j in order]
    blocks_in.wait()
    for number, (j, copy) in enumerate(zip(order, outward)):
        send_g[j] = grads[block_for(flip(me, j))]
        if number == 0:
            pl.semaphore_wait(barrier, groups - 1 + levels)
        copy.start()
    recv_g[0] = grads[block_for(me)]
    for load in loads:
        load.wait()

    def powers(m, carry):
        x = root[m]
        square = split(mm(x, x))
        fourth = split(mm3(square, square))
        hi, lo = split(mm(x, fourth[0]) + mm(x, fourth[1]))
        fifth_hi[m] = hi
        fifth_lo[m] = lo
        fac[m] = (5.0 * x.astype(jnp.float32) - mm3((hi, lo), split(fac[m]))) / 4.0
        return carry

    lax.fori_loop(0, 2 * per, powers, 0)
    for copy in outward:
        copy.wait_recv()

    for s in range(per):
        place = jnp.int32(0)
        for j in range(1, groups):
            source = flip(me, j)
            for k in range(per):
                place = jnp.where(targets[k, source] == me * per + s, j, place)
        owned[s] = recv_g[place]

    def buddy_copy(level_no, c):
        level = levels - 1 - level_no
        source = fresh if level_no == 0 else moved.at[level_no - 1]
        m, cut = c // CUTS, pl.multiple_of((c % CUTS) * rows, rows)
        return pltpu.make_async_remote_copy(
            src_ref=source.at[m, pl.ds(cut, rows)],
            dst_ref=moved.at[level_no, m, pl.ds(cut, rows)],
            send_sem=b_send.at[level_no, c],
            recv_sem=b_recv.at[level_no, c],
            device_id=(me, flip(rep, 1 << level)),
            device_id_type=MESH,
        )

    def along(left, right, dim):
        return lax.dot_general(
            left, right, (((1,), (dim,)), ((), ())), preferred_element_type=jnp.float32
        )

    def newton(m, s, block, first, count):
        part = pl.ds(first, count)
        near, far = (0, 1) if m % 2 == 0 else (1, 0)
        upper = along(fifth_hi[m, part], block, near) + along(fifth_lo[m, part], block, near)
        high, low = split(upper)
        moment = along(high, block, far) + along(low, block, far)
        new = fac[m, part] - moment / 4.0
        old = root[m, part].astype(jnp.float32)
        fresh[m, part] = jnp.where(refresh[s] == 1, new, old).astype(jnp.bfloat16)

    stores = []
    for s in range(per):
        block = owned[s]
        if s == 0:
            newton(0, 0, block, 0, AHEAD // 2 * rows)
            for c in range(AHEAD // 2):
                buddy_copy(0, c).start()
            newton(0, 0, block, AHEAD // 2 * rows, width - AHEAD // 2 * rows)
            for c in range(AHEAD // 2, AHEAD):
                buddy_copy(0, c).start()
        else:
            newton(2 * s, s, block, 0, width)
        newton(2 * s + 1, s, block, 0, width)
        half = mm(fresh[2 * s], block).astype(jnp.bfloat16)
        result[s] = mm(half, fresh[2 * s + 1]).astype(jnp.bfloat16)
        for side, out in enumerate((nleft_hbm, nright_hbm)):
            m = 2 * s + side
            stores.append(pltpu.make_async_copy(fresh.at[m], out.at[s], out_sem.at[m]))
            stores[-1].start()

    for j in [0] + order:
        index = jnp.int32(0)
        for k in range(per):
            there = targets[k, flip(me, j)]
            index = jnp.where(there // per == me, there % per, index)
        if j == 0:
            recv_r[0] = result[index]
        else:
            send_r[j] = result[index]
    backward = [exchange(send_r, recv_r, r_send, r_recv, j) for j in order]
    for copy in backward:
        copy.start()

    def buddy_store(c, wait):
        s, cut = c // (2 * CUTS), pl.multiple_of((c % CUTS) * rows, rows)
        for side, out in enumerate((bleft_hbm, bright_hbm)):

            @pl.when((c // CUTS) % 2 == side)
            def _():
                copy = pltpu.make_async_copy(
                    moved.at[levels - 1, 2 * s + side, pl.ds(cut, rows)],
                    out.at[s, pl.ds(cut, rows)],
                    buddy_out_sem.at[c],
                )
                if wait:
                    copy.wait()
                else:
                    copy.start()

    def step(t, carry):
        @pl.when(t < chunks)
        def _():
            buddy_copy(0, t).start()

        for n in range(levels):
            c = t - AHEAD - BEHIND * n

            @pl.when(jnp.logical_and(c >= 0, c < chunks))
            def _():
                buddy_copy(n, c).wait_recv()
                m, cut = c // CUTS, pl.multiple_of((c % CUTS) * rows, rows)
                level = levels - 1 - n
                crossing = (offset[0] // (1 << level)) % 2 == 1
                here = fresh if n == 0 else moved.at[n - 1]
                mine = here[m, pl.ds(cut, rows)].astype(jnp.float32)
                theirs = moved[n, m, pl.ds(cut, rows)].astype(jnp.float32)
                moved[n, m, pl.ds(cut, rows)] = jnp.where(crossing, theirs, mine).astype(
                    jnp.bfloat16
                )
                if n < levels - 1:
                    buddy_copy(n + 1, c).start()
                else:
                    buddy_store(c, False)

        return carry

    lax.fori_loop(AHEAD, chunks, step, 0)

    for copy in backward:
        copy.wait_recv()
    for k in range(per):
        place = jnp.int32(0)
        for j in range(1, groups):
            place = jnp.where(targets[k, me] // per == flip(me, j), j, place)
        home[k] = recv_r[place]
    stores.append(pltpu.make_async_copy(home, precond_hbm, out_sem.at[2 * per]))
    stores[-1].start()

    lax.fori_loop(chunks, chunks + AHEAD + BEHIND * (levels - 1), step, 0)

    for copy in stores:
        copy.wait()
    for copy in outward + backward:
        copy.wait_send()

    def drain(c, carry):
        for n in range(levels):
            buddy_copy(n, c).wait_send()
        buddy_store(c, True)
        return carry

    lax.fori_loop(0, chunks, drain, 0)


def hand_on(*refs):
    sources, targets, (stage, load_sem, store_sem) = refs[:5], refs[5:10], refs[10:]
    loads, stores = [], []
    for i in range(5):
        for s in range(sources[i].shape[0]):
            loads.append(
                pltpu.make_async_copy(sources[i].at[s], stage.at[i, s], load_sem.at[i, s])
            )
            stores.append(
                pltpu.make_async_copy(stage.at[i, s], targets[i].at[s], store_sem.at[i, s])
            )
    for load in loads:
        load.start()
    for load, store in zip(loads, stores):
        load.wait()
        store.start()
    for store in stores:
        store.wait()


def per_device(
    groups,
    replicas,
    grads,
    targets,
    left_factor,
    right_factor,
    left_root,
    right_root,
    refresh,
    buddy_offset,
):
    per, width = grads.shape[2], grads.shape[3]
    levels = replicas.bit_length() - 1
    chunks = 2 * per * CUTS
    shape = grads.shape
    blocks = (per, width, width)
    bf = jnp.bfloat16
    smem = pl.BlockSpec(memory_space=pltpu.SMEM)
    hbm = pl.BlockSpec(memory_space=pl.ANY)
    dma = pltpu.SemaphoreType.DMA
    matrices = (2 * per, width, width)
    slots = (groups, width, width)
    products = 2 * per * 10 + 2 * per
    outs = pl.pallas_call(
        functools.partial(kernel, groups, replicas),
        out_shape=[jax.ShapeDtypeStruct(blocks, bf)] * 5,
        in_specs=[smem, smem, smem, hbm, hbm, hbm, hbm, hbm],
        out_specs=[hbm] * 5,
        scratch_shapes=[
            pltpu.VMEM(blocks, bf),
            pltpu.VMEM(matrices, jnp.float32),
            pltpu.VMEM(matrices, bf),
            pltpu.VMEM(matrices, bf),
            pltpu.VMEM(matrices, bf),
            pltpu.VMEM(slots, bf),
            pltpu.VMEM(slots, bf),
            pltpu.VMEM(blocks, bf),
            pltpu.VMEM(matrices, bf),
            pltpu.VMEM(blocks, bf),
            pltpu.VMEM(slots, bf),
            pltpu.VMEM(slots, bf),
            pltpu.VMEM(blocks, bf),
            pltpu.VMEM((levels,) + matrices, bf),
            dma((3, 2 * per)),
            dma((2 * per + 1,)),
            dma((chunks,)),
            dma((groups,)),
            dma((groups,)),
            dma((groups,)),
            dma((groups,)),
            dma((levels, chunks)),
            dma((levels, chunks)),
        ],
        compiler_params=pltpu.CompilerParams(
            collective_id=0, has_side_effects=True, vmem_limit_bytes=56 * 1024 * 1024
        ),
        cost_estimate=pl.CostEstimate(
            flops=products * 2 * width**3, bytes_accessed=24 * per * width**2, transcendentals=0
        ),
        name="refresh_and_exchange",
    )(
        targets.transpose(1, 2, 0).reshape(per, groups),
        refresh.reshape(per),
        buddy_offset,
        grads.reshape(blocks),
        left_factor.reshape(blocks),
        right_factor.reshape(blocks),
        left_root.reshape(blocks),
        right_root.reshape(blocks),
    )
    outs = pl.pallas_call(
        hand_on,
        out_shape=[jax.ShapeDtypeStruct(blocks, bf)] * 5,
        in_specs=[hbm] * 5,
        out_specs=[hbm] * 5,
        scratch_shapes=[pltpu.VMEM((5,) + blocks, bf), dma((5, per)), dma((5, per))],
        name="hand_on",
    )(*outs)
    return tuple(out.reshape(shape) for out in outs)


def solution(mesh):
    blocks = P("fsdp", "rep", None, None, None)
    placed = (
        blocks,
        P(None, "rep", None),
        blocks,
        blocks,
        blocks,
        blocks,
        P("fsdp", "rep", None),
        P("fsdp"),
    )
    return jax.shard_map(
        functools.partial(per_device, mesh.shape["fsdp"], mesh.shape["rep"]),
        mesh=mesh,
        in_specs=placed,
        out_specs=(blocks,) * 5,
        check_vma=False,
    )
```

```python
import functools

import jax
import jax.numpy as jnp
from jax import lax
from jax.experimental import pallas as pl
from jax.experimental.pallas import tpu as pltpu
from jax.sharding import PartitionSpec as P

MESH = pl.DeviceIdType.MESH
CUTS = 8
AHEAD = 4
BEHIND = 3
KEPT = 4


def flip(index, mask):
    bit = 1
    while bit <= mask:
        if mask & bit:
            index = index + bit - 2 * bit * ((index // bit) % 2)
        bit *= 2
    return index


def mm(left, right):
    return jnp.dot(left, right, preferred_element_type=jnp.float32)


def split(value):
    high = value.astype(jnp.bfloat16)
    low = (value - high.astype(jnp.float32)).astype(jnp.bfloat16)
    return high, low


def mm3(left, right):
    (lh, ll), (rh, rl) = left, right
    return mm(lh, rh) + (mm(lh, rl) + mm(ll, rh))


def kernel(
    groups,
    replicas,
    targets,
    refresh,
    offset,
    grads_hbm,
    lfac_hbm,
    rfac_hbm,
    lroot_hbm,
    rroot_hbm,
    fresh_hbm,
    buddy_hbm,
    precond_hbm,
    grads,
    fac,
    root,
    fifth_hi,
    fifth_lo,
    send_g,
    recv_g,
    owned,
    fresh,
    result,
    send_r,
    recv_r,
    home,
    moved,
    in_sem,
    out_sem,
    buddy_out_sem,
    g_send,
    g_recv,
    r_send,
    r_recv,
    b_send,
    b_recv,
):
    per, width = grads.shape[0], grads.shape[1]
    me = lax.axis_index("fsdp")
    rep = lax.axis_index("rep")
    levels = replicas.bit_length() - 1
    rows = width // CUTS
    chunks = 2 * per * CUTS

    blocks_in = pltpu.make_async_copy(grads_hbm, grads, in_sem.at[2, 0])
    blocks_in.start()

    barrier = pltpu.get_barrier_semaphore()
    for j in range(1, groups):
        pl.semaphore_signal(barrier, inc=1, device_id=(flip(me, j), rep), device_id_type=MESH)
    for level in range(levels):
        pl.semaphore_signal(
            barrier, inc=1, device_id=(me, flip(rep, 1 << level)), device_id_type=MESH
        )

    loads = []
    for s in range(per):
        for side, (f_hbm, x_hbm) in enumerate(((lfac_hbm, lroot_hbm), (rfac_hbm, rroot_hbm))):
            m = 2 * s + side
            loads.append(pltpu.make_async_copy(x_hbm.at[s], root.at[m], in_sem.at[0, m]))
            loads.append(pltpu.make_async_copy(f_hbm.at[s], fac.at[m], in_sem.at[1, m]))
    for load in loads:
        load.start()

    def block_for(owner):
        index = jnp.int32(0)
        for k in range(1, per):
            index = jnp.where(targets[k, me] // per == owner, k, index)
        return index

    order = sorted(range(1, groups), key=lambda j: -bin(j).count("1"))
    def exchange(source, target, send_sem, recv_sem, j):
        return pltpu.make_async_remote_copy(
            src_ref=source.at[j],
            dst_ref=target.at[j],
            send_sem=send_sem.at[j],
            recv_sem=recv_sem.at[j],
            device_id=(flip(me, j), rep),
            device_id_type=MESH,
        )

    outward = [exchange(send_g, recv_g, g_send, g_recv, j) for j in order]
    blocks_in.wait()
    for number, (j, copy) in enumerate(zip(order, outward)):
        send_g[j] = grads[block_for(flip(me, j))]
        if number == 0:
            pl.semaphore_wait(barrier, groups - 1 + levels)
        copy.start()
    recv_g[0] = grads[block_for(me)]
    for load in loads:
        load.wait()

    def powers(m, carry):
        x = root[m]
        square = split(mm(x, x))
        fourth = split(mm3(square, square))
        hi, lo = split(mm(x, fourth[0]) + mm(x, fourth[1]))
        fifth_hi[m] = hi
        fifth_lo[m] = lo
        fac[m] = (5.0 * x.astype(jnp.float32) - mm3((hi, lo), split(fac[m]))) / 4.0
        return carry

    lax.fori_loop(0, 2 * per, powers, 0)
    for copy in outward:
        copy.wait_recv()

    for s in range(per):
        place = jnp.int32(0)
        for j in range(1, groups):
            source = flip(me, j)
            for k in range(per):
                place = jnp.where(targets[k, source] == me * per + s, j, place)
        owned[s] = recv_g[place]

    def buddy_copy(level_no, c):
        level = levels - 1 - level_no
        source = fresh if level_no == 0 else moved.at[level_no - 1]
        m, cut = c // CUTS, pl.multiple_of((c % CUTS) * rows, rows)
        return pltpu.make_async_remote_copy(
            src_ref=source.at[m, pl.ds(cut, rows)],
            dst_ref=moved.at[level_no, m, pl.ds(cut, rows)],
            send_sem=b_send.at[level_no, c],
            recv_sem=b_recv.at[level_no, c],
            device_id=(me, flip(rep, 1 << level)),
            device_id_type=MESH,
        )

    def along(left, right, dim):
        return lax.dot_general(
            left, right, (((1,), (dim,)), ((), ())), preferred_element_type=jnp.float32
        )

    def newton(m, s, block, first, count):
        part = pl.ds(first, count)
        near, far = (0, 1) if m % 2 == 0 else (1, 0)
        upper = along(fifth_hi[m, part], block, near) + along(fifth_lo[m, part], block, near)
        high, low = split(upper)
        moment = along(high, block, far) + along(low, block, far)
        new = fac[m, part] - moment / 4.0
        old = root[m, part].astype(jnp.float32)
        fresh[m, part] = jnp.where(refresh[s] == 1, new, old).astype(jnp.bfloat16)

    stores = []
    for s in range(per):
        block = owned[s]
        if s == 0:
            newton(0, 0, block, 0, AHEAD // 2 * rows)
            for c in range(AHEAD // 2):
                buddy_copy(0, c).start()
            newton(0, 0, block, AHEAD // 2 * rows, width - AHEAD // 2 * rows)
            for c in range(AHEAD // 2, AHEAD):
                buddy_copy(0, c).start()
        else:
            newton(2 * s, s, block, 0, width)
        newton(2 * s + 1, s, block, 0, width)
        half = mm(fresh[2 * s], block).astype(jnp.bfloat16)
        result[s] = mm(half, fresh[2 * s + 1]).astype(jnp.bfloat16)
        for m in (2 * s, 2 * s + 1):
            stores.append(pltpu.make_async_copy(fresh.at[m], fresh_hbm.at[m], out_sem.at[m]))
            stores[-1].start()

    for j in [0] + order:
        index = jnp.int32(0)
        for k in range(per):
            there = targets[k, flip(me, j)]
            index = jnp.where(there // per == me, there % per, index)
        if j == 0:
            recv_r[0] = result[index]
        else:
            send_r[j] = result[index]
    backward = [exchange(send_r, recv_r, r_send, r_recv, j) for j in order]
    for copy in backward:
        copy.start()

    def buddy_store(c):
        m, cut = c // CUTS, pl.multiple_of((c % CUTS) * rows, rows)
        part = (m, pl.ds(cut, rows))
        return pltpu.make_async_copy(
            moved.at[levels - 1].at[part], buddy_hbm.at[part], buddy_out_sem.at[c]
        )

    def step(t, carry):
        @pl.when(t < chunks)
        def _():
            buddy_copy(0, t).start()

        for n in range(levels):
            c = t - AHEAD - BEHIND * n

            @pl.when(jnp.logical_and(c >= 0, c < chunks))
            def _():
                buddy_copy(n, c).wait_recv()
                m, cut = c // CUTS, pl.multiple_of((c % CUTS) * rows, rows)
                level = levels - 1 - n
                crossing = (offset[0] // (1 << level)) % 2 == 1
                here = fresh if n == 0 else moved.at[n - 1]
                mine = here[m, pl.ds(cut, rows)].astype(jnp.float32)
                theirs = moved[n, m, pl.ds(cut, rows)].astype(jnp.float32)
                moved[n, m, pl.ds(cut, rows)] = jnp.where(crossing, theirs, mine).astype(
                    jnp.bfloat16
                )
                if n < levels - 1:
                    buddy_copy(n + 1, c).start()
                else:
                    buddy_store(c).start()
                    for earlier in range(levels):
                        buddy_copy(earlier, c).wait_send()

                    @pl.when(c >= KEPT)
                    def _():
                        buddy_store(c - KEPT).wait()

        return carry

    lax.fori_loop(AHEAD, chunks, step, 0)

    for copy in backward:
        copy.wait_recv()
    for k in range(per):
        place = jnp.int32(0)
        for j in range(1, groups):
            place = jnp.where(targets[k, me] // per == flip(me, j), j, place)
        home[k] = recv_r[place]
    stores.append(pltpu.make_async_copy(home, precond_hbm, out_sem.at[2 * per]))
    stores[-1].start()

    lax.fori_loop(chunks, chunks + AHEAD + BEHIND * (levels - 1), step, 0)

    for copy in stores:
        copy.wait()
    for copy in outward + backward:
        copy.wait_send()

    for c in range(chunks - KEPT, chunks):
        buddy_store(c).wait()


def hand_on(fresh, buddy, precond, nleft, nright, bleft, bright, home, stage, load_sem, store_sem):
    per = precond.shape[0]
    loads, stores = [], []
    plan = [(fresh, 0, nleft), (fresh, 1, nright), (buddy, 0, bleft), (buddy, 1, bright)]
    for i, (source, side, target) in enumerate(plan + [(precond, None, home)]):
        for s in range(per):
            block = s if side is None else 2 * s + side
            loads.append(
                pltpu.make_async_copy(source.at[block], stage.at[i, s], load_sem.at[i, s])
            )
            stores.append(
                pltpu.make_async_copy(stage.at[i, s], target.at[s], store_sem.at[i, s])
            )
    for load in loads:
        load.start()
    for load, store in zip(loads, stores):
        load.wait()
        store.start()
    for store in stores:
        store.wait()


def per_device(
    groups,
    replicas,
    grads,
    targets,
    left_factor,
    right_factor,
    left_root,
    right_root,
    refresh,
    buddy_offset,
):
    per, width = grads.shape[2], grads.shape[3]
    levels = replicas.bit_length() - 1
    chunks = 2 * per * CUTS
    shape = grads.shape
    blocks = (per, width, width)
    bf = jnp.bfloat16
    smem = pl.BlockSpec(memory_space=pltpu.SMEM)
    hbm = pl.BlockSpec(memory_space=pl.ANY)
    dma = pltpu.SemaphoreType.DMA
    matrices = (2 * per, width, width)
    slots = (groups, width, width)
    products = 2 * per * 10 + 2 * per
    outs = pl.pallas_call(
        functools.partial(kernel, groups, replicas),
        out_shape=[jax.ShapeDtypeStruct(dims, bf) for dims in (matrices, matrices, blocks)],
        in_specs=[smem, smem, smem, hbm, hbm, hbm, hbm, hbm],
        out_specs=[hbm] * 3,
        scratch_shapes=[
            pltpu.VMEM(blocks, bf),
            pltpu.VMEM(matrices, jnp.float32),
            pltpu.VMEM(matrices, bf),
            pltpu.VMEM(matrices, bf),
            pltpu.VMEM(matrices, bf),
            pltpu.VMEM(slots, bf),
            pltpu.VMEM(slots, bf),
            pltpu.VMEM(blocks, bf),
            pltpu.VMEM(matrices, bf),
            pltpu.VMEM(blocks, bf),
            pltpu.VMEM(slots, bf),
            pltpu.VMEM(slots, bf),
            pltpu.VMEM(blocks, bf),
            pltpu.VMEM((levels,) + matrices, bf),
            dma((3, 2 * per)),
            dma((2 * per + 1,)),
            dma((chunks,)),
            dma((groups,)),
            dma((groups,)),
            dma((groups,)),
            dma((groups,)),
            dma((levels, chunks)),
            dma((levels, chunks)),
        ],
        compiler_params=pltpu.CompilerParams(
            collective_id=0, has_side_effects=True, vmem_limit_bytes=56 * 1024 * 1024
        ),
        cost_estimate=pl.CostEstimate(
            flops=products * 2 * width**3, bytes_accessed=24 * per * width**2, transcendentals=0
        ),
        name="refresh_and_exchange",
    )(
        targets.transpose(1, 2, 0).reshape(per, groups),
        refresh.reshape(per),
        buddy_offset,
        grads.reshape(blocks),
        left_factor.reshape(blocks),
        right_factor.reshape(blocks),
        left_root.reshape(blocks),
        right_root.reshape(blocks),
    )
    outs = pl.pallas_call(
        hand_on,
        out_shape=[jax.ShapeDtypeStruct(blocks, bf)] * 5,
        in_specs=[hbm] * 3,
        out_specs=[hbm] * 5,
        scratch_shapes=[pltpu.VMEM((5,) + blocks, bf), dma((5, per)), dma((5, per))],
        name="hand_on",
    )(*outs)
    return tuple(out.reshape(shape) for out in outs)


def solution(mesh):
    blocks = P("fsdp", "rep", None, None, None)
    placed = (
        blocks,
        P(None, "rep", None),
        blocks,
        blocks,
        blocks,
        blocks,
        P("fsdp", "rep", None),
        P("fsdp"),
    )
    return jax.shard_map(
        functools.partial(per_device, mesh.shape["fsdp"], mesh.shape["rep"]),
        mesh=mesh,
        in_specs=placed,
        out_specs=(blocks,) * 5,
        check_vma=False,
    )
```

```python
import functools

import jax
import jax.numpy as jnp
from jax import lax
from jax.experimental import pallas as pl
from jax.experimental.pallas import tpu as pltpu
from jax.sharding import PartitionSpec as P

MESH = pl.DeviceIdType.MESH
CUTS = 8
AHEAD = 6
BEHIND = 4
KEPT = 4


def flip(index, mask):
    bit = 1
    while bit <= mask:
        if mask & bit:
            index = index + bit - 2 * bit * ((index // bit) % 2)
        bit *= 2
    return index


def mm(left, right):
    return jnp.dot(left, right, preferred_element_type=jnp.float32)


def split(value):
    high = value.astype(jnp.bfloat16)
    low = (value - high.astype(jnp.float32)).astype(jnp.bfloat16)
    return high, low


def mm3(left, right):
    (lh, ll), (rh, rl) = left, right
    return mm(lh, rh) + (mm(lh, rl) + mm(ll, rh))


def kernel(
    groups,
    replicas,
    targets,
    refresh,
    offset,
    grads_hbm,
    lfac_hbm,
    rfac_hbm,
    lroot_hbm,
    rroot_hbm,
    fresh_hbm,
    buddy_hbm,
    precond_hbm,
    grads,
    fac,
    root,
    fifth_hi,
    fifth_lo,
    send_g,
    recv_g,
    owned,
    fresh,
    result,
    send_r,
    recv_r,
    home,
    moved,
    in_sem,
    out_sem,
    buddy_out_sem,
    g_send,
    g_recv,
    r_send,
    r_recv,
    b_send,
    b_recv,
):
    per, width = grads.shape[0], grads.shape[1]
    me = lax.axis_index("fsdp")
    rep = lax.axis_index("rep")
    levels = replicas.bit_length() - 1
    rows = width // CUTS
    chunks = 2 * per * CUTS

    blocks_in = pltpu.make_async_copy(grads_hbm, grads, in_sem.at[2, 0])
    blocks_in.start()

    barrier = pltpu.get_barrier_semaphore()
    for j in range(1, groups):
        pl.semaphore_signal(barrier, inc=1, device_id=(flip(me, j), rep), device_id_type=MESH)
    for level in range(levels):
        pl.semaphore_signal(
            barrier, inc=1, device_id=(me, flip(rep, 1 << level)), device_id_type=MESH
        )

    loads = []
    for s in range(per):
        for side, (f_hbm, x_hbm) in enumerate(((lfac_hbm, lroot_hbm), (rfac_hbm, rroot_hbm))):
            m = 2 * s + side
            loads.append(pltpu.make_async_copy(x_hbm.at[s], root.at[m], in_sem.at[0, m]))
            loads.append(pltpu.make_async_copy(f_hbm.at[s], fac.at[m], in_sem.at[1, m]))
    for load in loads:
        load.start()

    def block_for(owner):
        index = jnp.int32(0)
        for k in range(1, per):
            index = jnp.where(targets[k, me] // per == owner, k, index)
        return index

    order = sorted(range(1, groups), key=lambda j: -bin(j).count("1"))
    def exchange(source, target, send_sem, recv_sem, j):
        return pltpu.make_async_remote_copy(
            src_ref=source.at[j],
            dst_ref=target.at[j],
            send_sem=send_sem.at[j],
            recv_sem=recv_sem.at[j],
            device_id=(flip(me, j), rep),
            device_id_type=MESH,
        )

    outward = [exchange(send_g, recv_g, g_send, g_recv, j) for j in order]
    blocks_in.wait()
    for number, (j, copy) in enumerate(zip(order, outward)):
        send_g[j] = grads[block_for(flip(me, j))]
        if number == 0:
            pl.semaphore_wait(barrier, groups - 1 + levels)
        copy.start()
    recv_g[0] = grads[block_for(me)]
    for load in loads:
        load.wait()

    def powers(m, carry):
        x = root[m]
        square = split(mm(x, x))
        fourth = split(mm3(square, square))
        hi, lo = split(mm(x, fourth[0]) + mm(x, fourth[1]))
        fifth_hi[m] = hi
        fifth_lo[m] = lo
        fac[m] = (5.0 * x.astype(jnp.float32) - mm3((hi, lo), split(fac[m]))) / 4.0
        return carry

    lax.fori_loop(0, 2 * per, powers, 0)
    for copy in outward:
        copy.wait_recv()

    for s in range(per):
        place = jnp.int32(0)
        for j in range(1, groups):
            source = flip(me, j)
            for k in range(per):
                place = jnp.where(targets[k, source] == me * per + s, j, place)
        owned[s] = recv_g[place]

    def routes(level_no):
        level = levels - 1 - level_no
        if levels > 1 and level_no < 2:
            return level, 2 * levels - 3 - level
        return level, level

    def buddy_copy(level_no, c):
        even, odd = routes(level_no)
        turn = c % 2
        device = flip(rep, 1 << even) * (1 - turn) + flip(rep, 1 << odd) * turn
        source = fresh if level_no == 0 else moved.at[level_no - 1]
        m, cut = c // CUTS, pl.multiple_of((c % CUTS) * rows, rows)
        return pltpu.make_async_remote_copy(
            src_ref=source.at[m, pl.ds(cut, rows)],
            dst_ref=moved.at[level_no, m, pl.ds(cut, rows)],
            send_sem=b_send.at[level_no, c],
            recv_sem=b_recv.at[level_no, c],
            device_id=(me, device),
            device_id_type=MESH,
        )

    def along(left, right, dim):
        return lax.dot_general(
            left, right, (((1,), (dim,)), ((), ())), preferred_element_type=jnp.float32
        )

    def newton(m, s, block, first, count):
        part = pl.ds(first, count)
        near, far = (0, 1) if m % 2 == 0 else (1, 0)
        upper = along(fifth_hi[m, part], block, near) + along(fifth_lo[m, part], block, near)
        high, low = split(upper)
        moment = along(high, block, far) + along(low, block, far)
        new = fac[m, part] - moment / 4.0
        old = root[m, part].astype(jnp.float32)
        fresh[m, part] = jnp.where(refresh[s] == 1, new, old).astype(jnp.bfloat16)

    stores = []
    for s in range(per):
        block = owned[s]
        if s == 0:
            newton(0, 0, block, 0, AHEAD // 2 * rows)
            for c in range(AHEAD // 2):
                buddy_copy(0, c).start()
            newton(0, 0, block, AHEAD // 2 * rows, width - AHEAD // 2 * rows)
            for c in range(AHEAD // 2, AHEAD):
                buddy_copy(0, c).start()
        else:
            newton(2 * s, s, block, 0, width)
        newton(2 * s + 1, s, block, 0, width)
        half = mm(fresh[2 * s], block).astype(jnp.bfloat16)
        result[s] = mm(half, fresh[2 * s + 1]).astype(jnp.bfloat16)
        for m in (2 * s, 2 * s + 1):
            stores.append(pltpu.make_async_copy(fresh.at[m], fresh_hbm.at[m], out_sem.at[m]))
            stores[-1].start()

    for j in [0] + order:
        index = jnp.int32(0)
        for k in range(per):
            there = targets[k, flip(me, j)]
            index = jnp.where(there // per == me, there % per, index)
        if j == 0:
            recv_r[0] = result[index]
        else:
            send_r[j] = result[index]
    backward = [exchange(send_r, recv_r, r_send, r_recv, j) for j in order]
    for copy in backward:
        copy.start()

    def buddy_store(c):
        m, cut = c // CUTS, pl.multiple_of((c % CUTS) * rows, rows)
        part = (m, pl.ds(cut, rows))
        return pltpu.make_async_copy(
            moved.at[levels - 1].at[part], buddy_hbm.at[part], buddy_out_sem.at[c]
        )

    def step(t, carry):
        @pl.when(t < chunks)
        def _():
            buddy_copy(0, t).start()

        for n in range(levels):
            c = t - AHEAD - BEHIND * n

            @pl.when(jnp.logical_and(c >= 0, c < chunks))
            def _():
                buddy_copy(n, c).wait_recv()
                m, cut = c // CUTS, pl.multiple_of((c % CUTS) * rows, rows)
                even, odd = [(offset[0] // (1 << level)) % 2 for level in routes(n)]
                crossing = jnp.where(c % 2 == 0, even, odd) == 1
                here = fresh if n == 0 else moved.at[n - 1]
                mine = here[m, pl.ds(cut, rows)].astype(jnp.float32)
                theirs = moved[n, m, pl.ds(cut, rows)].astype(jnp.float32)
                moved[n, m, pl.ds(cut, rows)] = jnp.where(crossing, theirs, mine).astype(
                    jnp.bfloat16
                )
                if n < levels - 1:
                    buddy_copy(n + 1, c).start()
                else:
                    buddy_store(c).start()
                    for earlier in range(levels):
                        buddy_copy(earlier, c).wait_send()

                    @pl.when(c >= KEPT)
                    def _():
                        buddy_store(c - KEPT).wait()

        return carry

    lax.fori_loop(AHEAD, chunks, step, 0)

    for copy in backward:
        copy.wait_recv()
    for k in range(per):
        place = jnp.int32(0)
        for j in range(1, groups):
            place = jnp.where(targets[k, me] // per == flip(me, j), j, place)
        home[k] = recv_r[place]
    stores.append(pltpu.make_async_copy(home, precond_hbm, out_sem.at[2 * per]))
    stores[-1].start()

    lax.fori_loop(chunks, chunks + AHEAD + BEHIND * (levels - 1), step, 0)

    for copy in stores:
        copy.wait()
    for copy in outward + backward:
        copy.wait_send()

    for c in range(chunks - KEPT, chunks):
        buddy_store(c).wait()


def hand_on(fresh, buddy, precond, nleft, nright, bleft, bright, home, stage, load_sem, store_sem):
    per = precond.shape[0]
    loads, stores = [], []
    plan = [(fresh, 0, nleft), (fresh, 1, nright), (buddy, 0, bleft), (buddy, 1, bright)]
    for i, (source, side, target) in enumerate(plan + [(precond, None, home)]):
        for s in range(per):
            block = s if side is None else 2 * s + side
            loads.append(
                pltpu.make_async_copy(source.at[block], stage.at[i, s], load_sem.at[i, s])
            )
            stores.append(
                pltpu.make_async_copy(stage.at[i, s], target.at[s], store_sem.at[i, s])
            )
    for load in loads:
        load.start()
    for load, store in zip(loads, stores):
        load.wait()
        store.start()
    for store in stores:
        store.wait()


def per_device(
    groups,
    replicas,
    grads,
    targets,
    left_factor,
    right_factor,
    left_root,
    right_root,
    refresh,
    buddy_offset,
):
    per, width = grads.shape[2], grads.shape[3]
    levels = replicas.bit_length() - 1
    chunks = 2 * per * CUTS
    shape = grads.shape
    blocks = (per, width, width)
    bf = jnp.bfloat16
    smem = pl.BlockSpec(memory_space=pltpu.SMEM)
    hbm = pl.BlockSpec(memory_space=pl.ANY)
    dma = pltpu.SemaphoreType.DMA
    matrices = (2 * per, width, width)
    slots = (groups, width, width)
    products = 2 * per * 10 + 2 * per
    outs = pl.pallas_call(
        functools.partial(kernel, groups, replicas),
        out_shape=[jax.ShapeDtypeStruct(dims, bf) for dims in (matrices, matrices, blocks)],
        in_specs=[smem, smem, smem, hbm, hbm, hbm, hbm, hbm],
        out_specs=[hbm] * 3,
        scratch_shapes=[
            pltpu.VMEM(blocks, bf),
            pltpu.VMEM(matrices, jnp.float32),
            pltpu.VMEM(matrices, bf),
            pltpu.VMEM(matrices, bf),
            pltpu.VMEM(matrices, bf),
            pltpu.VMEM(slots, bf),
            pltpu.VMEM(slots, bf),
            pltpu.VMEM(blocks, bf),
            pltpu.VMEM(matrices, bf),
            pltpu.VMEM(blocks, bf),
            pltpu.VMEM(slots, bf),
            pltpu.VMEM(slots, bf),
            pltpu.VMEM(blocks, bf),
            pltpu.VMEM((levels,) + matrices, bf),
            dma((3, 2 * per)),
            dma((2 * per + 1,)),
            dma((chunks,)),
            dma((groups,)),
            dma((groups,)),
            dma((groups,)),
            dma((groups,)),
            dma((levels, chunks)),
            dma((levels, chunks)),
        ],
        compiler_params=pltpu.CompilerParams(
            collective_id=0, has_side_effects=True, vmem_limit_bytes=56 * 1024 * 1024
        ),
        cost_estimate=pl.CostEstimate(
            flops=products * 2 * width**3, bytes_accessed=24 * per * width**2, transcendentals=0
        ),
        name="refresh_and_exchange",
    )(
        targets.transpose(1, 2, 0).reshape(per, groups),
        refresh.reshape(per),
        buddy_offset,
        grads.reshape(blocks),
        left_factor.reshape(blocks),
        right_factor.reshape(blocks),
        left_root.reshape(blocks),
        right_root.reshape(blocks),
    )
    outs = pl.pallas_call(
        hand_on,
        out_shape=[jax.ShapeDtypeStruct(blocks, bf)] * 5,
        in_specs=[hbm] * 3,
        out_specs=[hbm] * 5,
        scratch_shapes=[pltpu.VMEM((5,) + blocks, bf), dma((5, per)), dma((5, per))],
        name="hand_on",
    )(*outs)
    return tuple(out.reshape(shape) for out in outs)


def solution(mesh):
    blocks = P("fsdp", "rep", None, None, None)
    placed = (
        blocks,
        P(None, "rep", None),
        blocks,
        blocks,
        blocks,
        blocks,
        P("fsdp", "rep", None),
        P("fsdp"),
    )
    return jax.shard_map(
        functools.partial(per_device, mesh.shape["fsdp"], mesh.shape["rep"]),
        mesh=mesh,
        in_specs=placed,
        out_specs=(blocks,) * 5,
        check_vma=False,
    )
```
